32 devices in a mesh: row: 4 (over x, core), col: 8 (over z, y).
Axes of the slice: x: 2, y: 2, z: 4, core: 2. Of those that a mesh axis runs over, the one named last changes fastest.
Arguments:
- frames: bfloat16 [1536, 4096], P('row', 'col'), may hold values from -6 to 6
- gain: float32 [4096], replicated, may hold values from 0.3 to 10
- w_value: bfloat16 [4096, 4096], P('row', 'col'), may hold values from -0.09375 to 0.09375
- w_gate: bfloat16 [4096, 4096], P('row', 'col'), may hold values from -0.09375 to 0.09375
- kernel: float32 [31, 4096], P(None, 'col'), may hold values from -1.5 to 1.5
- bias: float32 [4096], P('col'), may hold values from -3 to 3
- w_out: bfloat16 [4096, 4096], P('row', 'col'), may hold values from -0.09375 to 0.09375
- grad_out: bfloat16 [1536, 4096], P('row', 'col'), may hold values from -6 to 6
Outputs:
- encoded: bfloat16 [1536, 4096], P('row', 'col')
- input_grad: bfloat16 [1536, 4096], P('row', 'col')
- grad_value: float32 [4096, 4096], P('row', 'col')
- grad_gate: float32 [4096, 4096], P('row', 'col')
- grad_kernel: float32 [31, 4096], P(None, 'col')
- grad_bias: float32 [4096], P('col')
- grad_out_weight: float32 [4096, 4096], P('row', 'col')
- grad_gain: float32 [4096], P('col')
The draws below stay inside these ranges and needn't reach their ends.
All inputs are finite; a program needn't handle non-finite values.
Results may differ from the reference program's by a relative error of at most 0.035.
Values may be sent and summed in bfloat16 or wider, within the bound.
A program may use at most 128 MiB of HBM per device.

```python
import math
import jax
import jax.numpy as jnp
from jax import lax

D = 4096
F = 4096
K = 31
LEN = 2048
TOTAL = 1536
N_COL = 8


def draw_gain(key, part):
    place = jnp.arange(D, dtype=jnp.float32) / D
    rough = jnp.exp(jax.random.uniform(jax.random.fold_in(key, 11), (D,), jnp.float32, math.log(0.7), math.log(1.5)))
    ramp = jnp.exp(math.log(4.0) * place)
    return (0.5 * ramp * rough).astype(jnp.float32)


def block_scale(own_key, extent, cuts, smallest, high):
    def one(dim, blocks):
        draws = jax.random.uniform(jax.random.fold_in(jax.random.fold_in(own_key, 6), dim), (blocks,), jnp.float32, smallest / len(cuts), high / len(cuts))
        return jnp.repeat(jnp.exp(draws), extent[dim] // blocks).reshape((-1,) + (1,) * (len(extent) - dim - 1))

    loudness = one(*cuts[0])
    for cut in cuts[1:]:
        loudness = loudness * one(*cut)
    return loudness


def gaussian(key, dims, scale, bound, cuts=(), kind=jnp.bfloat16):
    array = scale * jax.random.normal(key, dims, jnp.float32)
    if cuts:
        array = array * block_scale(key, dims, cuts, -0.22, 0.18)
    return jnp.clip(array, -bound, bound).astype(kind)


def setup_inputs(seed: int = 0) -> dict:
    keys = jax.random.split(jax.random.key(seed), 9)
    return {
        "frames": gaussian(keys[0], (TOTAL, D), 1.0, 6.0, ((0, 4), (1, 8))),
        "gain": draw_gain(jax.random.fold_in(keys[8], 71), 0),
        "w_value": gaussian(keys[2], (D, F), D ** -0.5, 0.09375, ((0, 4), (1, 8))),
        "w_gate": gaussian(keys[3], (D, F), D ** -0.5, 0.09375, ((0, 4), (1, 8))),
        "kernel": gaussian(keys[4], (K, F), 0.25, 1.5, ((1, 8),), jnp.float32),
        "bias": gaussian(keys[5], (F,), 0.5, 3.0, ((0, 8),), jnp.float32),
        "w_out": gaussian(keys[6], (F, D), F ** -0.5, 0.09375, ((0, 4), (1, 8))),
        "grad_out": gaussian(keys[7], (TOTAL, D), 1.0, 6.0, ((0, 4), (1, 8))),
    }


epsilon = 1e-05

def tap_masks(positions):
    offsets = jnp.arange(K, dtype=jnp.int32) - K // 2
    placed = (positions % LEN)[None, :] + offsets[:, None]
    return ((placed >= 0) & (placed < LEN)).astype(jnp.float32)

def contract_rows(left, right):
    return lax.dot_general(left, right, (((0,), (0,)), ((), ())), preferred_element_type=jnp.float32)

def contract_cols(left, right):
    return lax.dot_general(left, right, (((1,), (1,)), ((), ())), preferred_element_type=jnp.float32)

def reference(frames, gain, w_value, w_gate, kernel, bias, w_out, grad_out):
    total = frames.shape[0]
    width = frames.shape[1]
    channels = w_value.shape[1]
    half_width = K // 2
    wide = frames.astype(jnp.float32)
    mean_row = lax.optimization_barrier(jnp.sum(wide, axis=1)) / width
    inv_std = lax.rsqrt(lax.optimization_barrier(jnp.sum(wide * wide, axis=1)) / width - mean_row * mean_row + epsilon)
    centred = (wide - mean_row[:, None]) * inv_std[:, None]
    normed = (centred * gain[None, :]).astype(jnp.bfloat16)
    value_pre = jnp.dot(normed, w_value, preferred_element_type=jnp.float32)
    gate_pre = jnp.dot(normed, w_gate, preferred_element_type=jnp.float32)
    gate_sig = jax.nn.sigmoid(gate_pre)
    gated = (value_pre * gate_sig).astype(jnp.bfloat16)
    masks = tap_masks(jnp.arange(total, dtype=jnp.int32))
    padded_glu = jnp.pad(gated.astype(jnp.float32), ((half_width, half_width), (0, 0)))
    conv_pre = jnp.zeros((total, channels), jnp.float32) + bias[None, :]
    for tap_index in range(K):
        conv_pre = conv_pre + kernel[tap_index][None, :] * masks[tap_index][:, None] * padded_glu[tap_index:tap_index + total]
    conv_sig = jax.nn.sigmoid(conv_pre)
    activated = (conv_pre * conv_sig).astype(jnp.bfloat16)
    encoded = (wide + jnp.dot(activated, w_out, preferred_element_type=jnp.float32)).astype(jnp.bfloat16)
    feat_block = width // N_COL

    def act_step(carry, index):
        grad_part = lax.dynamic_slice_in_dim(grad_out, index * feat_block, feat_block, 1)
        weight_part = lax.dynamic_slice_in_dim(w_out, index * feat_block, feat_block, 1)
        part = contract_cols(grad_part, weight_part)
        return (carry + lax.optimization_barrier(part.astype(jnp.bfloat16)).astype(jnp.float32), None)
    act_grad, unused = lax.scan(act_step, jnp.zeros((total, channels), jnp.float32), jnp.arange(N_COL, dtype=jnp.int32))
    grad_out_weight = contract_rows(activated, grad_out)
    conv_grad = (act_grad * conv_sig * (1.0 + conv_pre * (1.0 - conv_sig))).astype(jnp.bfloat16)
    conv_wide = conv_grad.astype(jnp.float32)
    glu_grad = jnp.zeros((total, channels), jnp.float32)
    kernel_rows = []
    for tap_index in range(K):
        masked = jnp.pad(masks[tap_index][:, None] * conv_wide, ((half_width, half_width), (0, 0)))
        begin = 2 * half_width - tap_index
        glu_grad = glu_grad + kernel[tap_index][None, :] * masked[begin:begin + total]
        kernel_rows.append(lax.optimization_barrier(jnp.sum(masks[tap_index][:, None] * conv_wide * padded_glu[tap_index:tap_index + total], axis=0)))
    grad_kernel = jnp.stack(kernel_rows)
    grad_bias = lax.optimization_barrier(jnp.sum(conv_wide, axis=0))
    value_grad = (glu_grad * gate_sig).astype(jnp.bfloat16)
    gate_grad = (glu_grad * value_pre * gate_sig * (1.0 - gate_sig)).astype(jnp.bfloat16)
    grad_value = contract_rows(normed, value_grad)
    grad_gate = contract_rows(normed, gate_grad)
    chan_block = channels // N_COL

    def norm_step(carry, index):
        value_part = lax.dynamic_slice_in_dim(value_grad, index * chan_block, chan_block, 1)
        gate_part = lax.dynamic_slice_in_dim(gate_grad, index * chan_block, chan_block, 1)
        wv_part = lax.dynamic_slice_in_dim(w_value, index * chan_block, chan_block, 1)
        wg_part = lax.dynamic_slice_in_dim(w_gate, index * chan_block, chan_block, 1)
        part = contract_cols(value_part, wv_part) + contract_cols(gate_part, wg_part)
        return (carry + lax.optimization_barrier(part.astype(jnp.bfloat16)).astype(jnp.float32), None)
    normed_grad, unused = lax.scan(norm_step, jnp.zeros((total, width), jnp.float32), jnp.arange(N_COL, dtype=jnp.int32))
    hat_grad = normed_grad * gain[None, :]
    first_sum = lax.optimization_barrier(jnp.sum(hat_grad, axis=1)) / width
    second_sum = lax.optimization_barrier(jnp.sum(hat_grad * centred, axis=1)) / width
    input_grad = (grad_out.astype(jnp.float32) + inv_std[:, None] * (hat_grad - first_sum[:, None] - centred * second_sum[:, None])).astype(jnp.bfloat16)
    grad_gain = lax.optimization_barrier(jnp.sum(normed_grad * centred, axis=0))
    return (encoded, input_grad, grad_value, grad_gate, grad_kernel, grad_bias, grad_out_weight, grad_gain)
```

```python
import jax
import jax.numpy as jnp
from jax import lax
from jax.experimental import pallas as pl
from jax.experimental.pallas import tpu as pltpu
from jax.sharding import PartitionSpec as P

K = 31
LEN = 2048
HALF = K // 2
epsilon = 1e-05
MESH = pl.DeviceIdType.MESH
ANY = pl.BlockSpec(memory_space=pl.ANY)
VMEM = pl.BlockSpec(memory_space=pltpu.VMEM)
DMA = pltpu.SemaphoreType.DMA


def send(src, dst, sent, arrived, row, col):
    return pltpu.make_async_remote_copy(
        src_ref=src,
        dst_ref=dst,
        send_sem=sent,
        recv_sem=arrived,
        device_id=(row, col),
        device_id_type=MESH,
    )


def await_bytes(ref, sem):
    pltpu.make_async_copy(ref, ref, sem).wait()


def span(index, size):
    if isinstance(index, int):
        return pl.ds(index * size, size)
    return pl.ds(pl.multiple_of(index * size, size), size)


def by_rows(rows, cols, body):
    chunk = max(16, min(rows, 16384 // cols))
    while rows % chunk:
        chunk -= 16

    @pl.loop(0, rows // chunk)
    def _(step):
        body(span(step, chunk))


class Spread:
    memory = ANY

    def __init__(self, n, m, block, by_frames, dtype=jnp.bfloat16):
        self.n, self.m, self.block, self.by_frames = n, m, block, by_frames
        a, b = block
        whole = (n * a, m * b) if by_frames else (a, n * m * b)
        self.out_shape = [jax.ShapeDtypeStruct(whole, dtype)]
        self.out_specs = [ANY]
        self.in_specs = [ANY]
        self.scratch = [DMA((n, m)), DMA((2 + m, n)), DMA]
        self.phases = n + 2

    def part(self, ref, k, y):
        a, b = self.block
        if self.by_frames:
            return ref.at[span(k, a), span(y, b)]
        return ref.at[:, span(y * self.n + k, b)]

    def run(self, phase, refs):
        x, out, arrived, sent, first = refs
        n, m = self.n, self.m
        r, c = lax.axis_index("row"), lax.axis_index("col")
        z, y = c // m, c % m

        def moves(k):
            mine = self.part(out, k, y)

            def up():
                return send(mine, mine, sent.at[0, k], arrived.at[k, y], r, lax.rem(c + m, n * m))

            def down():
                return send(mine, mine, sent.at[1, k], arrived.at[k, y], r, lax.rem(c + n * m - m, n * m))

            def side(d):
                return send(mine, mine, sent.at[1 + d, k], arrived.at[k, y], r, z * m + lax.rem(y + d, m))

            return up, down, side

        goes_up = jnp.logical_and(z >= r, z < n - 1)
        goes_down = jnp.logical_and(z <= r, z > 0)
        if phase == 0:
            home = self.part(out, r, y)

            @pl.when(r == z)
            def _():
                pltpu.make_async_copy(x, home, arrived.at[r, y]).start()

            @pl.when(r != z)
            def _():
                send(x, home, first, arrived.at[r, y], z, c).start()
        elif phase <= n:
            k = phase - 1
            await_bytes(self.part(out, k, y), arrived.at[k, y])
            up, down, side = moves(k)

            @pl.when(goes_up)
            def _():
                up().start()

            @pl.when(goes_down)
            def _():
                down().start()

            for d in range(1, m):
                side(d).start()
        else:
            for k in range(n):
                for d in range(1, m):
                    other = lax.rem(y + d, m)
                    await_bytes(self.part(out, k, other), arrived.at[k, other])
            for k in range(n):
                up, down, side = moves(k)

                @pl.when(goes_up)
                def _():
                    up().wait_send()

                @pl.when(goes_down)
                def _():
                    down().wait_send()

                for d in range(1, m):
                    side(d).wait_send()

            @pl.when(r != z)
            def _():
                send(x, self.part(out, r, y), first, arrived.at[r, y], z, c).wait_send()


class Fold:
    def __init__(self, n, m, block, by_frames):
        self.n, self.m, self.block, self.by_frames = n, m, block, by_frames
        self.out_shape = [jax.ShapeDtypeStruct(block, jnp.bfloat16)]
        self.out_specs = [VMEM]
        self.in_specs = [VMEM]
        self.scratch = [
            pltpu.VMEM((n, m) + block, jnp.bfloat16),
            pltpu.VMEM((2, n) + block, jnp.bfloat16),
            pltpu.VMEM((n,) + block, jnp.bfloat16),
            pltpu.VMEM(block, jnp.float32),
            DMA((n, m)),
            DMA((n, m)),
            DMA((2, n)),
            DMA((n,)),
            DMA,
        ]
        self.phases = n + 2

    part = Spread.part

    def run(self, phase, refs):
        parts, out, ybuf, zbuf, sbuf, acc, ysent, ycame, zcame, zsent, ocame = refs
        n, m = self.n, self.m
        a, b = self.block
        r, c = lax.axis_index("row"), lax.axis_index("col")
        z, y = c // m, c % m
        lower, upper = lax.rem(c + n * m - m, n * m), lax.rem(c + m, n * m)

        def side(k, d):
            other = lax.rem(y + d, m)
            return send(
                self.part(parts, k, other), ybuf.at[k, y], ysent.at[k, d], ycame.at[k, y], r, z * m + other
            )

        def onward(k):
            def down():
                return send(sbuf.at[k], zbuf.at[0, k], zsent.at[k], zcame.at[0, k], r, lower)

            def up():
                return send(sbuf.at[k], zbuf.at[1, k], zsent.at[k], zcame.at[1, k], r, upper)

            def home():
                return send(sbuf.at[k], out, zsent.at[k], ocame, k, c)

            return down, up, home

        if phase == 0:
            for k in range(n):
                for d in range(1, m):
                    side(k, d).start()
        elif phase <= n:
            k = phase - 1
            for d in range(1, m):
                other = lax.rem(y + d, m)
                await_bytes(ybuf.at[k, other], ycame.at[k, other])
            mine = self.part(parts, k, y)

            def first(rows):
                total = mine[rows, :].astype(jnp.float32)
                for d in range(1, m):
                    total = total + ybuf[k, lax.rem(y + d, m), rows, :].astype(jnp.float32)
                acc[rows, :] = total

            by_rows(a, b, first)
            for which, ready in (
                (0, jnp.logical_and(z >= r, z < n - 1)),
                (1, jnp.logical_and(z <= r, z > 0)),
            ):

                @pl.when(ready)
                def _():
                    await_bytes(zbuf.at[which, k], zcame.at[which, k])

                    def add(rows):
                        acc[rows, :] = acc[rows, :] + zbuf[which, k, rows, :].astype(jnp.float32)

                    by_rows(a, b, add)

            def last(rows):
                sbuf[k, rows, :] = acc[rows, :].astype(jnp.bfloat16)

            by_rows(a, b, last)
            down, up, home = onward(k)

            @pl.when(z > r)
            def _():
                down().start()

            @pl.when(z < r)
            def _():
                up().start()

            @pl.when(jnp.logical_and(z == r, r != k))
            def _():
                home().start()

            @pl.when(jnp.logical_and(z == r, r == k))
            def _():
                def keep(rows):
                    out[rows, :] = sbuf[k, rows, :]

                by_rows(a, b, keep)
        else:

            @pl.when(z != r)
            def _():
                await_bytes(out, ocame)

            for k in range(n):
                for d in range(1, m):
                    side(k, d).wait_send()
                down, up, home = onward(k)

                @pl.when(jnp.logical_or(z != r, r != k))
                def _():
                    down().wait_send()


class RowFold:
    def __init__(self, n, block, by_frames, count):
        self.n, self.block, self.by_frames, self.count = n, block, by_frames, count
        half = n // 2
        self.out_shape = [jax.ShapeDtypeStruct(block, jnp.float32)] * count
        self.out_specs = [VMEM] * count
        self.in_specs = [VMEM] * count
        buf = pltpu.VMEM((count, half) + block, jnp.bfloat16)
        sem = DMA((count, half))
        self.scratch = [buf, buf, buf, sem, sem, sem, sem]
        self.phases = 3

    def part(self, ref, k):
        a, b = self.block
        return ref.at[span(k, a), :] if self.by_frames else ref.at[:, span(k, b)]

    def run(self, phase, refs):
        count = self.count
        parts, outs = refs[:count], refs[count : 2 * count]
        near, far, sums, nsent, ncame, fsent, fcame = refs[2 * count :]
        n = self.n
        half = n // 2
        a, b = self.block
        r, c = lax.axis_index("row"), lax.axis_index("col")
        x, core = r // 2, r % 2
        sibling = x * 2 + 1 - core

        def to_sibling(j, d):
            g = lax.rem(x + d, half)
            return send(
                self.part(parts[j], g * 2 + 1 - core), near.at[j, g], nsent.at[j, g], ncame.at[j, g], sibling, c
            )

        def across(j, d):
            g = lax.rem(x + d, half)
            return send(sums.at[j, g], far.at[j, x], fsent.at[j, g], fcame.at[j, x], g * 2 + core, c)

        order = list(range(1, half)) + [0]
        if phase == 0:
            for d in order:
                for j in range(count):
                    to_sibling(j, d).start()
        elif phase == 1:
            for d in range(1, half):
                g = lax.rem(x + d, half)
                for j in range(count):
                    await_bytes(near.at[j, g], ncame.at[j, g])
                    mine = self.part(parts[j], g * 2 + core)

                    def add(rows):
                        sums[j, g, rows, :] = (
                            mine[rows, :].astype(jnp.float32) + near[j, g, rows, :].astype(jnp.float32)
                        ).astype(jnp.bfloat16)

                    by_rows(a, b, add)
                    across(j, d).start()
        else:
            for j in range(count):
                await_bytes(near.at[j, x], ncame.at[j, x])
                for d in range(1, half):
                    g = lax.rem(x + d, half)
                    await_bytes(far.at[j, g], fcame.at[j, g])
                mine = self.part(parts[j], r)

                def total(rows):
                    value = mine[rows, :].astype(jnp.float32) + near[j, x, rows, :].astype(jnp.float32)
                    for d in range(1, half):
                        value = value + far[j, lax.rem(x + d, half), rows, :].astype(jnp.float32)
                    outs[j][rows, :] = value

                by_rows(a, b, total)
            for j in range(count):
                for d in order:
                    to_sibling(j, d).wait_send()
                for d in range(1, half):
                    across(j, d).wait_send()


class RowGather:
    def __init__(self, n, block, by_frames, count):
        self.n, self.block, self.by_frames, self.count = n, block, by_frames, count
        a, b = block
        whole = (n * a, b) if by_frames else (a, n * b)
        half = n // 2
        self.out_shape = [jax.ShapeDtypeStruct(whole, jnp.bfloat16)] * count
        self.out_specs = [ANY] * count
        self.in_specs = [ANY] * count
        self.scratch = [DMA((count, n)), DMA((count, half)), DMA((count, half)), DMA((count,))]
        self.phases = 3

    part = RowFold.part

    def run(self, phase, refs):
        count = self.count
        xs, outs = refs[:count], refs[count : 2 * count]
        came, fsent, nsent, kept = refs[2 * count :]
        n = self.n
        half = n // 2
        r, c = lax.axis_index("row"), lax.axis_index("col")
        x, core = r // 2, r % 2
        sibling = x * 2 + 1 - core

        def keep(j):
            return pltpu.make_async_copy(xs[j], self.part(outs[j], r), kept.at[j])

        def across(j, d):
            g = lax.rem(x + d, half)
            return send(xs[j], self.part(outs[j], r), fsent.at[j, d], came.at[j, r], g * 2 + core, c)

        def to_sibling(j, d):
            g = lax.rem(x + d, half)
            block = self.part(outs[j], g * 2 + core)
            source = xs[j] if d == 0 else block
            return send(source, block, nsent.at[j, d], came.at[j, g * 2 + core], sibling, c)

        if phase == 0:
            for j in range(count):
                for d in range(1, half):
                    across(j, d).start()
                to_sibling(j, 0).start()
                keep(j).start()
        elif phase == 1:
            for d in range(1, half):
                g = lax.rem(x + d, half)
                for j in range(count):
                    await_bytes(self.part(outs[j], g * 2 + core), came.at[j, g * 2 + core])
                    to_sibling(j, d).start()
        else:
            for j in range(count):
                for d in range(half):
                    g = lax.rem(x + d, half)
                    await_bytes(self.part(outs[j], g * 2 + 1 - core), came.at[j, g * 2 + 1 - core])
                keep(j).wait()
                for d in range(1, half):
                    across(j, d).wait_send()
                for d in range(half):
                    to_sibling(j, d).wait_send()


def greet(n, m):
    r, c = lax.axis_index("row"), lax.axis_index("col")
    z, y = c // m, c % m
    barrier = pltpu.get_barrier_semaphore()

    def hello(row, col):
        pl.semaphore_signal(barrier, inc=1, device_id=(row, col), device_id_type=MESH)

    for d in range(1, n):
        hello(lax.rem(r + d, n), c)
    for d in range(1, m):
        hello(r, z * m + lax.rem(y + d, m))

    @pl.when(z > 0)
    def _():
        hello(r, c - m)

    @pl.when(z < n - 1)
    def _():
        hello(r, c + m)

    lower, upper = (z + n - 1) // n, (2 * n - 2 - z) // n
    pl.semaphore_wait(barrier, (n - 1) + (m - 1) + lower + upper)


def exchange(n, m, ident, moves, operands):
    in_specs = [s for mv in moves for s in mv.in_specs]
    out_specs = [s for mv in moves for s in mv.out_specs]
    out_shape = [s for mv in moves for s in mv.out_shape]
    scratch = [s for mv in moves for s in mv.scratch]

    def body(*refs):
        ins = refs[: len(in_specs)]
        outs = refs[len(in_specs) : len(in_specs) + len(out_specs)]
        rest = refs[len(in_specs) + len(out_specs) :]
        own = []
        i = o = s = 0
        for mv in moves:
            own.append(
                tuple(ins[i : i + len(mv.in_specs)])
                + tuple(outs[o : o + len(mv.out_specs)])
                + tuple(rest[s : s + len(mv.scratch)])
            )
            i, o, s = i + len(mv.in_specs), o + len(mv.out_specs), s + len(mv.scratch)
        greet(n, m)
        for phase in range(max(mv.phases for mv in moves)):
            for mv, mine in zip(moves, own):
                if phase < mv.phases:
                    mv.run(phase, mine)

    return pl.pallas_call(
        body,
        out_shape=out_shape,
        in_specs=in_specs,
        out_specs=out_specs,
        scratch_shapes=scratch,
        compiler_params=pltpu.CompilerParams(
            collective_id=ident, has_side_effects=True, vmem_limit_bytes=50 * 2**20
        ),
        cost_estimate=pl.CostEstimate(flops=0, bytes_accessed=100_000_000, transcendentals=0),
    )(*operands)


def dot(left, right, contract):
    return lax.dot_general(left, right, ((contract[:1], contract[1:]), ((), ())), preferred_element_type=jnp.float32)


def clips(total):
    return [(start, min(start + LEN, total)) for start in range(0, total, LEN)]


def padded(block):
    return jnp.pad(block, ((HALF, HALF), (0, 0)))


def shards(frames, gain, w_value, w_gate, kernel, bias, w_out, grad_out):
    n, n_col = lax.axis_size("row"), lax.axis_size("col")
    m = n_col // n
    rows, feats = frames.shape
    depth, chans = w_value.shape
    total, width = rows * n, feats * n_col
    own = chans // n
    r, c = lax.axis_index("row"), lax.axis_index("col")

    wide = frames.astype(jnp.float32)
    sums = jnp.stack([jnp.sum(wide, axis=1), jnp.sum(wide * wide, axis=1)])
    sums = lax.all_gather(sums, ("row", "col"), axis=0, tiled=False)
    sums = jnp.sum(sums.reshape(n, n_col, 2, rows), axis=1)
    frames_full, grad_full = exchange(
        n,
        m,
        1,
        [Spread(n, m, (rows, feats), True), RowGather(n, (rows, feats), True, 1)],
        (frames, grad_out),
    )
    mean = sums[:, 0].reshape(total) / width
    inv_std = lax.rsqrt(sums[:, 1].reshape(total) / width - mean * mean + epsilon)
    gain_row = lax.dynamic_slice_in_dim(gain, r * depth, depth, 0)
    normed = (
        (frames_full.astype(jnp.float32) - mean[:, None]) * inv_std[:, None] * gain_row[None, :]
    ).astype(jnp.bfloat16)
    value_part = dot(normed, w_value, (1, 0)).astype(jnp.bfloat16)
    gate_part = dot(normed, w_gate, (1, 0)).astype(jnp.bfloat16)
    act_part = dot(grad_full, w_out, (1, 1)).astype(jnp.bfloat16)
    scaled = jnp.stack(
        [
            jnp.sum(w_value.astype(jnp.float32) * gain_row[:, None], axis=0),
            jnp.sum(w_gate.astype(jnp.float32) * gain_row[:, None], axis=0),
        ]
    )
    scaled = lax.psum(scaled, "row")
    scaled = lax.dynamic_slice_in_dim(scaled, r * own, own, 1)

    value_pre, gate_pre, act_grad = exchange(
        n,
        m,
        2,
        [RowFold(n, (total, own), False, 2), Fold(n, m, (total, own), False)],
        (value_part, gate_part, act_part),
    )
    gate_sig = jax.nn.sigmoid(gate_pre)
    gated = (value_pre * gate_sig).astype(jnp.bfloat16).astype(jnp.float32)
    taps = lax.dynamic_slice_in_dim(kernel, r * own, own, 1)
    own_bias = lax.dynamic_slice_in_dim(bias, r * own, own, 0)
    conv_parts, glu_parts = [], []
    for begin, end in clips(total):
        ahead = padded(gated[begin:end])
        conv = jnp.zeros((end - begin, own), jnp.float32) + own_bias[None, :]
        for k in range(K):
            conv = conv + taps[k][None, :] * ahead[k : k + end - begin]
        conv_parts.append(conv)
    conv_pre = jnp.concatenate(conv_parts, axis=0)
    conv_sig = jax.nn.sigmoid(conv_pre)
    activated = (conv_pre * conv_sig).astype(jnp.bfloat16)
    conv_grad = (
        act_grad.astype(jnp.float32) * conv_sig * (1.0 + conv_pre * (1.0 - conv_sig))
    ).astype(jnp.bfloat16)
    conv_wide = conv_grad.astype(jnp.float32)
    tap_grads = jnp.zeros((K, own), jnp.float32)
    for begin, end in clips(total):
        back = padded(conv_wide[begin:end])
        ahead = padded(gated[begin:end])
        glu = jnp.zeros((end - begin, own), jnp.float32)
        tap_rows = []
        for k in range(K):
            glu = glu + taps[k][None, :] * back[2 * HALF - k : 2 * HALF - k + end - begin]
            tap_rows.append(jnp.sum(conv_wide[begin:end] * ahead[k : k + end - begin], axis=0))
        glu_parts.append(glu)
        tap_grads = tap_grads + jnp.stack(tap_rows)
    glu_grad = jnp.concatenate(glu_parts, axis=0)
    value_grad = (glu_grad * gate_sig).astype(jnp.bfloat16)
    gate_grad = (glu_grad * value_pre * gate_sig * (1.0 - gate_sig)).astype(jnp.bfloat16)
    bias_grad = jnp.sum(conv_wide, axis=0)
    depthwise = lax.all_gather(
        jnp.concatenate([tap_grads, bias_grad[None, :]], axis=0), "row", axis=1, tiled=True
    )
    value_wide, gate_wide = value_grad.astype(jnp.float32), gate_grad.astype(jnp.float32)
    norm_sums = jnp.stack(
        [
            jnp.sum(value_wide * scaled[0][None, :] + gate_wide * scaled[1][None, :], axis=1),
            jnp.sum(value_wide * value_pre + gate_wide * gate_pre, axis=1),
        ]
    )
    norm_sums = lax.psum(norm_sums, ("row", "col"))

    act_full, value_full, gate_full = exchange(
        n,
        m,
        3,
        [Spread(n, m, (total, own), False), RowGather(n, (total, own), False, 2)],
        (activated, value_grad, gate_grad),
    )
    out_part = dot(act_full, w_out, (1, 0)).astype(jnp.bfloat16)
    norm_part = (dot(value_full, w_value, (1, 1)) + dot(gate_full, w_gate, (1, 1))).astype(jnp.bfloat16)
    out_sum, normed_grad = exchange(
        n,
        m,
        4,
        [RowFold(n, (rows, feats), True, 1), Fold(n, m, (rows, feats), True)],
        (out_part, norm_part),
    )
    grad_value = dot(normed, value_full, (0, 0))
    grad_gate = dot(normed, gate_full, (0, 0))
    grad_out_weight = dot(act_full, grad_full, (0, 0))
    gain_part = (
        jnp.sum(w_value.astype(jnp.float32) * grad_value + w_gate.astype(jnp.float32) * grad_gate, axis=1) / gain_row
    )
    gain_part = lax.all_gather(lax.psum(gain_part, "col"), "row", axis=0, tiled=True)
    grad_gain = lax.dynamic_slice_in_dim(gain_part, c * feats, feats, 0)

    encoded = (wide + out_sum).astype(jnp.bfloat16)
    local_mean = lax.dynamic_slice_in_dim(mean, r * rows, rows, 0)
    local_inv = lax.dynamic_slice_in_dim(inv_std, r * rows, rows, 0)
    local_sums = lax.dynamic_slice_in_dim(norm_sums, r * rows, rows, 1) / width
    centred = (wide - local_mean[:, None]) * local_inv[:, None]
    local_gain = lax.dynamic_slice_in_dim(gain, c * feats, feats, 0)
    hat_grad = normed_grad.astype(jnp.float32) * local_gain[None, :]
    input_grad = (
        grad_out.astype(jnp.float32)
        + local_inv[:, None] * (hat_grad - local_sums[0][:, None] - centred * local_sums[1][:, None])
    ).astype(jnp.bfloat16)
    return (
        encoded,
        input_grad,
        grad_value,
        grad_gate,
        depthwise[:K],
        depthwise[K],
        grad_out_weight,
        grad_gain,
    )


def extended(block, sides, width):
    for axis, dim in sides:
        count = lax.axis_size(axis)
        forward = [(i, i + 1) for i in range(count - 1)]
        backward = [(target, source) for source, target in forward]
        low = lax.ppermute(
            lax.slice_in_dim(block, block.shape[dim] - width, None, axis=dim), axis, forward
        )
        high = lax.ppermute(lax.slice_in_dim(block, 0, width, axis=dim), axis, backward)
        block = jnp.concatenate([low, block, high], axis=dim)
    return block


def tap_masks(positions):
    offsets = jnp.arange(K, dtype=jnp.int32) - K // 2
    placed = (positions % LEN)[None, :] + offsets[:, None]
    return ((placed >= 0) & (placed < LEN)).astype(jnp.float32)


def contract_rows(left, right):
    return lax.dot_general(
        left, right, (((0,), (0,)), ((), ())), preferred_element_type=jnp.float32
    )


def contract_cols(left, right):
    return lax.dot_general(
        left, right, (((1,), (1,)), ((), ())), preferred_element_type=jnp.float32
    )


def narrow_shards(frames, gain, w_value, w_gate, kernel, bias, w_out, grad_out):
    row_count = frames.shape[0]
    col_count = frames.shape[1]
    chan_count = w_value.shape[1]
    width = col_count * lax.axis_size("col")
    half_width = K // 2
    row_start = lax.axis_index("row") * row_count
    col_start = lax.axis_index("col") * col_count
    local_gain = lax.dynamic_slice_in_dim(gain, col_start, col_count, 0)
    wide = frames.astype(jnp.float32)
    sum_row, square_sum = lax.psum((jnp.sum(wide, axis=1), jnp.sum(wide * wide, axis=1)), "col")
    mean_row = sum_row / width
    inv_std = lax.rsqrt(square_sum / width - mean_row * mean_row + epsilon)
    centred = (wide - mean_row[:, None]) * inv_std[:, None]
    normed = lax.all_gather(
        (centred * local_gain[None, :]).astype(jnp.bfloat16), "col", axis=1, tiled=True
    )
    value_full, gate_full = (
        lax.all_gather(w_value, "row", axis=0, tiled=True),
        lax.all_gather(w_gate, "row", axis=0, tiled=True),
    )
    value_pre = jnp.dot(normed, value_full, preferred_element_type=jnp.float32)
    gate_pre = jnp.dot(normed, gate_full, preferred_element_type=jnp.float32)
    gate_sig = jax.nn.sigmoid(gate_pre)
    gated = (value_pre * gate_sig).astype(jnp.bfloat16)
    padded_glu = extended(gated, (("row", 0),), half_width).astype(jnp.float32)
    local_masks = tap_masks(row_start + jnp.arange(row_count, dtype=jnp.int32))
    conv_pre = jnp.zeros((row_count, chan_count), jnp.float32) + bias[None, :]
    for tap_index in range(K):
        conv_pre = (
            conv_pre
            + kernel[tap_index][None, :]
            * local_masks[tap_index][:, None]
            * padded_glu[tap_index : tap_index + row_count]
        )
    conv_sig = jax.nn.sigmoid(conv_pre)
    activated = (conv_pre * conv_sig).astype(jnp.bfloat16)
    act_full = lax.all_gather(activated, "col", axis=1, tiled=True)
    out_full = lax.all_gather(w_out, "row", axis=0, tiled=True)
    encoded = (
        frames.astype(jnp.float32) + jnp.dot(act_full, out_full, preferred_element_type=jnp.float32)
    ).astype(jnp.bfloat16)
    act_terms = contract_cols(grad_out, out_full)
    act_grad = lax.psum_scatter(
        act_terms.astype(jnp.bfloat16), "col", scatter_dimension=1, tiled=True
    ).astype(jnp.float32)
    grad_out_weight = lax.psum_scatter(
        contract_rows(act_full, grad_out).astype(jnp.bfloat16),
        "row",
        scatter_dimension=0,
        tiled=True,
    ).astype(jnp.float32)
    conv_grad = (act_grad * conv_sig * (1.0 + conv_pre * (1.0 - conv_sig))).astype(jnp.bfloat16)
    conv_wide = conv_grad.astype(jnp.float32)
    padded_grad = extended(conv_grad, (("row", 0),), half_width).astype(jnp.float32)
    outer_masks = tap_masks(
        row_start - half_width + jnp.arange(row_count + 2 * half_width, dtype=jnp.int32)
    )
    glu_grad = jnp.zeros((row_count, chan_count), jnp.float32)
    kernel_rows = []
    for tap_index in range(K):
        begin = 2 * half_width - tap_index
        glu_grad = (
            glu_grad
            + kernel[tap_index][None, :]
            * outer_masks[tap_index, begin : begin + row_count][:, None]
            * padded_grad[begin : begin + row_count]
        )
        kernel_rows.append(
            jnp.sum(
                local_masks[tap_index][:, None]
                * conv_wide
                * padded_glu[tap_index : tap_index + row_count],
                axis=0,
            )
        )
    kernel_term = jnp.stack(kernel_rows)
    bias_term = jnp.sum(conv_wide, axis=0)
    grad_kernel, grad_bias = lax.psum((kernel_term, bias_term), "row")
    value_grad = (glu_grad * gate_sig).astype(jnp.bfloat16)
    gate_grad = (glu_grad * value_pre * gate_sig * (1.0 - gate_sig)).astype(jnp.bfloat16)
    both_grads = jnp.concatenate([value_grad, gate_grad], axis=1)
    in_weight = lax.psum_scatter(
        contract_rows(normed, both_grads).astype(jnp.bfloat16),
        "row",
        scatter_dimension=0,
        tiled=True,
    ).astype(jnp.float32)
    grad_value = in_weight[:, :chan_count]
    grad_gate = in_weight[:, chan_count:]
    norm_terms = contract_cols(value_grad, value_full) + contract_cols(gate_grad, gate_full)
    normed_grad = lax.psum_scatter(
        norm_terms.astype(jnp.bfloat16), "col", scatter_dimension=1, tiled=True
    ).astype(jnp.float32)
    hat_grad = normed_grad * local_gain[None, :]
    first_sum, second_sum = lax.psum(
        (jnp.sum(hat_grad, axis=1), jnp.sum(hat_grad * centred, axis=1)), "col"
    )
    input_grad = (
        grad_out.astype(jnp.float32)
        + inv_std[:, None]
        * (hat_grad - first_sum[:, None] / width - centred * (second_sum / width)[:, None])
    ).astype(jnp.bfloat16)
    gain_term = jnp.sum(normed_grad * centred, axis=0)
    grad_gain = lax.psum(gain_term, "row")
    return (
        encoded,
        input_grad,
        grad_value,
        grad_gate,
        grad_kernel,
        grad_bias,
        grad_out_weight,
        grad_gain,
    )


def choose(frames, gain, w_value, *others):
    fits = w_value.shape[1] % (128 * lax.axis_size("row")) == 0 and lax.axis_size("col") % lax.axis_size("row") == 0
    return (shards if fits else narrow_shards)(frames, gain, w_value, *others)


def solution(mesh):
    tile = P("row", "col")
    return jax.shard_map(
        choose,
        mesh=mesh,
        in_specs=(tile, P(), tile, tile, P(None, "col"), P("col"), tile, tile),
        out_specs=(tile, tile, tile, tile, P(None, "col"), P("col"), tile, P("col")),
        check_vma=False,
    )
```

```python
import jax
import jax.numpy as jnp
from jax import lax
from jax.experimental import pallas as pl
from jax.experimental.pallas import tpu as pltpu
from jax.sharding import PartitionSpec as P

K = 31
LEN = 2048
HALF = K // 2
epsilon = 1e-05
MESH = pl.DeviceIdType.MESH
ANY = pl.BlockSpec(memory_space=pl.ANY)
VMEM = pl.BlockSpec(memory_space=pltpu.VMEM)
DMA = pltpu.SemaphoreType.DMA


def send(src, dst, sent, arrived, row, col):
    return pltpu.make_async_remote_copy(
        src_ref=src,
        dst_ref=dst,
        send_sem=sent,
        recv_sem=arrived,
        device_id=(row, col),
        device_id_type=MESH,
    )


def await_bytes(ref, sem):
    pltpu.make_async_copy(ref, ref, sem).wait()


def span(index, size):
    if isinstance(index, int):
        return pl.ds(index * size, size)
    return pl.ds(pl.multiple_of(index * size, size), size)


def by_rows(rows, cols, body):
    chunk = max(16, min(rows, 16384 // cols))
    while rows % chunk:
        chunk -= 16

    @pl.loop(0, rows // chunk)
    def _(step):
        body(span(step, chunk))


class Spread:
    def __init__(self, n, m, block, by_frames, cuts):
        self.n, self.m, self.block, self.by_frames, self.cuts = n, m, block, by_frames, cuts
        a, b = block
        whole = (n * a, m * b) if by_frames else (a, n * m * b)
        self.out_shape = [jax.ShapeDtypeStruct(whole, jnp.bfloat16)]
        self.out_specs = [ANY]
        self.in_specs = [ANY]
        self.scratch = [DMA((n, cuts, m)), DMA((2 + m, n * cuts)), DMA((cuts,))]
        self.phases = n * cuts + 2

    def part(self, ref, k, y, cut):
        a, b = self.block
        high = a // self.cuts
        if self.by_frames:
            return ref.at[span(k * self.cuts + cut, high), span(y, b)]
        return ref.at[span(cut, high), span(y * self.n + k, b)]

    def run(self, phase, refs):
        x, out, arrived, sent, first = refs
        n, m, cuts = self.n, self.m, self.cuts
        r, c = lax.axis_index("row"), lax.axis_index("col")
        z, y = c // m, c % m

        def moves(q):
            k, cut = q // cuts, q % cuts
            mine = self.part(out, k, y, cut)
            came = arrived.at[k, cut, y]

            def up():
                return send(mine, mine, sent.at[0, q], came, r, lax.rem(c + m, n * m))

            def down():
                return send(mine, mine, sent.at[1, q], came, r, lax.rem(c + n * m - m, n * m))

            def side(d):
                return send(mine, mine, sent.at[1 + d, q], came, r, z * m + lax.rem(y + d, m))

            return up, down, side

        def own(cut):
            return x.at[span(cut, self.block[0] // cuts), :]

        def home(cut):
            return send(own(cut), self.part(out, r, y, cut), first.at[cut], arrived.at[r, cut, y], z, c)

        goes_up = jnp.logical_and(z >= r, z < n - 1)
        goes_down = jnp.logical_and(z <= r, z > 0)
        if phase == 0:

            @pl.when(r == z)
            def _():
                for cut in range(cuts):
                    pltpu.make_async_copy(own(cut), self.part(out, r, y, cut), arrived.at[r, cut, y]).start()

            @pl.when(r != z)
            def _():
                for cut in range(cuts):
                    home(cut).start()
        elif phase <= n * cuts:
            q = phase - 1
            await_bytes(self.part(out, q // cuts, y, q % cuts), arrived.at[q // cuts, q % cuts, y])
            up, down, side = moves(q)

            @pl.when(goes_up)
            def _():
                up().start()

            @pl.when(goes_down)
            def _():
                down().start()

            for d in range(1, m):
                side(d).start()
        else:
            for q in range(n * cuts):
                for d in range(1, m):
                    other = lax.rem(y + d, m)
                    await_bytes(self.part(out, q // cuts, other, q % cuts), arrived.at[q // cuts, q % cuts, other])
            for q in range(n * cuts):
                up, down, side = moves(q)

                @pl.when(goes_up)
                def _():
                    up().wait_send()

                @pl.when(goes_down)
                def _():
                    down().wait_send()

                for d in range(1, m):
                    side(d).wait_send()

            @pl.when(r != z)
            def _():
                for cut in range(cuts):
                    home(cut).wait_send()


class Fold:
    window = 3

    def __init__(self, n, m, block, by_frames, cuts):
        self.n, self.m, self.block, self.by_frames, self.cuts = n, m, block, by_frames, cuts
        self.out_shape = [jax.ShapeDtypeStruct(block, jnp.bfloat16)]
        self.out_specs = [VMEM]
        self.in_specs = [VMEM]
        piece = (block[0] // cuts, block[1])
        count = n * cuts
        self.scratch = [
            pltpu.VMEM((count, m) + piece, jnp.bfloat16),
            pltpu.VMEM((2, count) + piece, jnp.bfloat16),
            pltpu.VMEM((count,) + piece, jnp.bfloat16),
            DMA((count, m)),
            DMA((count, m)),
            DMA((2, count)),
            DMA((count,)),
            DMA((cuts,)),
        ]
        self.phases = count + 2

    part = Spread.part

    def run(self, phase, refs):
        parts, out, ybuf, zbuf, sbuf, ysent, ycame, zcame, zsent, ocame = refs
        n, m, cuts = self.n, self.m, self.cuts
        a, b = self.block
        high = a // cuts
        r, c = lax.axis_index("row"), lax.axis_index("col")
        z, y = c // m, c % m
        lower, upper = lax.rem(c + n * m - m, n * m), lax.rem(c + m, n * m)

        def side(q, d):
            other = lax.rem(y + d, m)
            mine = self.part(parts, q // cuts, other, q % cuts)
            return send(mine, ybuf.at[q, y], ysent.at[q, d], ycame.at[q, y], r, z * m + other)

        def onward(q):
            def down():
                return send(sbuf.at[q], zbuf.at[0, q], zsent.at[q], zcame.at[0, q], r, lower)

            def up():
                return send(sbuf.at[q], zbuf.at[1, q], zsent.at[q], zcame.at[1, q], r, upper)

            def home():
                cut = q % cuts
                return send(sbuf.at[q], out.at[span(cut, high), :], zsent.at[q], ocame.at[cut], q // cuts, c)

            return down, up, home

        if phase == 0:
            for q in range(min(self.window, n * cuts)):
                for d in range(1, m):
                    side(q, d).start()
        elif phase <= n * cuts:
            q = phase - 1
            k, cut = q // cuts, q % cuts
            for d in range(1, m):
                other = lax.rem(y + d, m)
                await_bytes(ybuf.at[q, other], ycame.at[q, other])
                side(q, d).wait_send()
                if q + self.window < n * cuts:
                    side(q + self.window, d).start()
            mine = self.part(parts, k, y, cut)

            def add(which):
                for w in which:
                    await_bytes(zbuf.at[w, q], zcame.at[w, q])

                def body(rows):
                    total = mine[rows, :].astype(jnp.float32)
                    for d in range(1, m):
                        total = total + ybuf[q, lax.rem(y + d, m), rows, :].astype(jnp.float32)
                    for w in which:
                        total = total + zbuf[w, q, rows, :].astype(jnp.float32)
                    sbuf[q, rows, :] = total.astype(jnp.bfloat16)

                by_rows(high, b, body)

            above = jnp.logical_and(z >= r, z < n - 1)
            below = jnp.logical_and(z <= r, z > 0)

            @pl.when(jnp.logical_and(above, below))
            def _():
                add((0, 1))

            @pl.when(jnp.logical_and(above, jnp.logical_not(below)))
            def _():
                add((0,))

            @pl.when(jnp.logical_and(jnp.logical_not(above), below))
            def _():
                add((1,))

            @pl.when(jnp.logical_not(jnp.logical_or(above, below)))
            def _():
                add(())

            down, up, home = onward(q)

            @pl.when(z > r)
            def _():
                down().start()

            @pl.when(z < r)
            def _():
                up().start()

            @pl.when(jnp.logical_and(z == r, r != k))
            def _():
                home().start()

            @pl.when(jnp.logical_and(z == r, r == k))
            def _():
                def keep(rows):
                    out.at[span(cut, high), :][rows, :] = sbuf[q, rows, :]

                by_rows(high, b, keep)
        else:

            @pl.when(z != r)
            def _():
                for cut in range(cuts):
                    await_bytes(out.at[span(cut, high), :], ocame.at[cut])

            for q in range(n * cuts):
                down, up, home = onward(q)

                @pl.when(jnp.logical_or(z != r, r != q // cuts))
                def _():
                    down().wait_send()


class Small:
    def __init__(self, n, n_col, block, over_col):
        self.n, self.n_col, self.over_col = n, n_col, over_col
        self.out_shape = [jax.ShapeDtypeStruct((n,) + block, jnp.float32)]
        self.out_specs = [VMEM]
        self.in_specs = [VMEM]
        self.scratch = [
            pltpu.VMEM((n_col,) + block, jnp.float32),
            pltpu.VMEM(block, jnp.float32),
            DMA((n_col,)),
            DMA((n_col,)),
            DMA((n,)),
            DMA((n,)),
        ]
        self.phases = 3

    def run(self, phase, refs):
        x, out, slots, total, csent, ccame, rsent, rcame = refs
        n, n_col = self.n, self.n_col
        r, c = lax.axis_index("row"), lax.axis_index("col")

        def to_col(d):
            return send(x, slots.at[c], csent.at[d], ccame.at[c], r, lax.rem(c + d, n_col))

        def to_row(d):
            return send(total, out.at[r], rsent.at[d], rcame.at[r], lax.rem(r + d, n), c)

        if phase == 0:
            if self.over_col:
                for d in range(1, n_col):
                    to_col(d).start()
        elif phase == 1:
            if self.over_col:
                slots[c] = x[...]
                for d in range(1, n_col):
                    other = lax.rem(c + d, n_col)
                    await_bytes(slots.at[other], ccame.at[other])
                value = slots[0]
                for j in range(1, n_col):
                    value = value + slots[j]
                total[...] = value
            else:
                total[...] = x[...]
            for d in range(1, n):
                to_row(d).start()
            out[r] = total[...]
        else:
            for d in range(1, n):
                other = lax.rem(r + d, n)
                await_bytes(out.at[other], rcame.at[other])
            for d in range(1, n):
                to_row(d).wait_send()
            if self.over_col:
                for d in range(1, n_col):
                    to_col(d).wait_send()


class RowFold:
    def __init__(self, n, block, by_frames, count):
        self.n, self.block, self.by_frames, self.count = n, block, by_frames, count
        half = n // 2
        self.out_shape = [jax.ShapeDtypeStruct(block, jnp.float32)] * count
        self.out_specs = [VMEM] * count
        self.in_specs = [VMEM] * count
        buf = pltpu.VMEM((count, half) + block, jnp.bfloat16)
        sem = DMA((count, half))
        self.scratch = [buf, buf, buf, sem, sem, sem, sem]
        self.phases = 3

    def part(self, ref, k):
        a, b = self.block
        return ref.at[span(k, a), :] if self.by_frames else ref.at[:, span(k, b)]

    def run(self, phase, refs):
        count = self.count
        parts, outs = refs[:count], refs[count : 2 * count]
        near, far, sums, nsent, ncame, fsent, fcame = refs[2 * count :]
        n = self.n
        half = n // 2
        a, b = self.block
        r, c = lax.axis_index("row"), lax.axis_index("col")
        x, core = r // 2, r % 2
        sibling = x * 2 + 1 - core

        def to_sibling(j, d):
            g = lax.rem(x + d, half)
            return send(
                self.part(parts[j], g * 2 + 1 - core), near.at[j, g], nsent.at[j, g], ncame.at[j, g], sibling, c
            )

        def across(j, d):
            g = lax.rem(x + d, half)
            return send(sums.at[j, g], far.at[j, x], fsent.at[j, g], fcame.at[j, x], g * 2 + core, c)

        order = list(range(1, half)) + [0]
        if phase == 0:
            for d in order:
                for j in range(count):
                    to_sibling(j, d).start()
        elif phase == 1:
            for d in range(1, half):
                g = lax.rem(x + d, half)
                for j in range(count):
                    await_bytes(near.at[j, g], ncame.at[j, g])
                    mine = self.part(parts[j], g * 2 + core)

                    def add(rows):
                        sums[j, g, rows, :] = (
                            mine[rows, :].astype(jnp.float32) + near[j, g, rows, :].astype(jnp.float32)
                        ).astype(jnp.bfloat16)

                    by_rows(a, b, add)
                    across(j, d).start()
        else:
            for j in range(count):
                await_bytes(near.at[j, x], ncame.at[j, x])
                for d in range(1, half):
                    g = lax.rem(x + d, half)
                    await_bytes(far.at[j, g], fcame.at[j, g])
                mine = self.part(parts[j], r)

                def total(rows):
                    value = mine[rows, :].astype(jnp.float32) + near[j, x, rows, :].astype(jnp.float32)
                    for d in range(1, half):
                        value = value + far[j, lax.rem(x + d, half), rows, :].astype(jnp.float32)
                    outs[j][rows, :] = value

                by_rows(a, b, total)
            for j in range(count):
                for d in order:
                    to_sibling(j, d).wait_send()
                for d in range(1, half):
                    across(j, d).wait_send()


class RowGather:
    late = True

    def __init__(self, n, block, by_frames, count):
        self.n, self.block, self.by_frames, self.count = n, block, by_frames, count
        a, b = block
        whole = (n * a, b) if by_frames else (a, n * b)
        half = n // 2
        self.out_shape = [jax.ShapeDtypeStruct(whole, jnp.bfloat16)] * count
        self.out_specs = [ANY] * count
        self.in_specs = [ANY] * count
        self.scratch = [DMA((count, n)), DMA((count, half)), DMA((count, half)), DMA((count,))]
        self.phases = 3

    part = RowFold.part

    def run(self, phase, refs):
        count = self.count
        xs, outs = refs[:count], refs[count : 2 * count]
        came, fsent, nsent, kept = refs[2 * count :]
        n = self.n
        half = n // 2
        r, c = lax.axis_index("row"), lax.axis_index("col")
        x, core = r // 2, r % 2
        sibling = x * 2 + 1 - core

        def keep(j):
            return pltpu.make_async_copy(xs[j], self.part(outs[j], r), kept.at[j])

        def across(j, d):
            g = lax.rem(x + d, half)
            return send(xs[j], self.part(outs[j], r), fsent.at[j, d], came.at[j, r], g * 2 + core, c)

        def to_sibling(j, d):
            g = lax.rem(x + d, half)
            block = self.part(outs[j], g * 2 + core)
            source = xs[j] if d == 0 else block
            return send(source, block, nsent.at[j, d], came.at[j, g * 2 + core], sibling, c)

        if phase == 0:
            for j in range(count):
                for d in range(1, half):
                    across(j, d).start()
                to_sibling(j, 0).start()
                keep(j).start()
        elif phase == 1:
            for d in range(1, half):
                g = lax.rem(x + d, half)
                for j in range(count):
                    await_bytes(self.part(outs[j], g * 2 + core), came.at[j, g * 2 + core])
                    to_sibling(j, d).start()
        else:
            for j in range(count):
                for d in range(half):
                    g = lax.rem(x + d, half)
                    await_bytes(self.part(outs[j], g * 2 + 1 - core), came.at[j, g * 2 + 1 - core])
                keep(j).wait()
                for d in range(1, half):
                    across(j, d).wait_send()
                for d in range(half):
                    to_sibling(j, d).wait_send()


def greet(n, n_col):
    r, c = lax.axis_index("row"), lax.axis_index("col")
    barrier = pltpu.get_barrier_semaphore()

    def hello(row, col):
        pl.semaphore_signal(barrier, inc=1, device_id=(row, col), device_id_type=MESH)

    for d in range(1, n):
        hello(lax.rem(r + d, n), c)
    for d in range(1, n_col):
        hello(r, lax.rem(c + d, n_col))
    pl.semaphore_wait(barrier, n - 1 + n_col - 1)


def exchange(n, m, ident, moves, operands):
    in_specs = [s for mv in moves for s in mv.in_specs]
    out_specs = [s for mv in moves for s in mv.out_specs]
    out_shape = [s for mv in moves for s in mv.out_shape]
    scratch = [s for mv in moves for s in mv.scratch]

    def body(*refs):
        ins = refs[: len(in_specs)]
        outs = refs[len(in_specs) : len(in_specs) + len(out_specs)]
        rest = refs[len(in_specs) + len(out_specs) :]
        own = []
        i = o = s = 0
        for mv in moves:
            own.append(
                tuple(ins[i : i + len(mv.in_specs)])
                + tuple(outs[o : o + len(mv.out_specs)])
                + tuple(rest[s : s + len(mv.scratch)])
            )
            i, o, s = i + len(mv.in_specs), o + len(mv.out_specs), s + len(mv.scratch)
        greet(n, n * m)
        steps = max(mv.phases for mv in moves)
        for step in range(steps):
            for mv, mine in zip(moves, own):
                late = getattr(mv, "late", False) and steps > mv.phases
                at = {0: 0, (steps // 2 if late else 1): 1, steps - 1: 2}
                if mv.phases == steps:
                    mv.run(step, mine)
                elif step in at:
                    mv.run(at[step], mine)

    return pl.pallas_call(
        body,
        out_shape=out_shape,
        in_specs=in_specs,
        out_specs=out_specs,
        scratch_shapes=scratch,
        compiler_params=pltpu.CompilerParams(
            collective_id=ident, has_side_effects=True, vmem_limit_bytes=50 * 2**20
        ),
        cost_estimate=pl.CostEstimate(flops=0, bytes_accessed=100_000_000, transcendentals=0),
    )(*operands)


def dot(left, right, contract):
    return lax.dot_general(left, right, ((contract[:1], contract[1:]), ((), ())), preferred_element_type=jnp.float32)


def eight(block):
    return jnp.pad(block, ((0, 8 - block.shape[0]), (0, 0)))


def clips(total):
    return [(start, min(start + LEN, total)) for start in range(0, total, LEN)]


def padded(block):
    return jnp.pad(block, ((HALF, HALF), (0, 0)))


def shards(frames, gain, w_value, w_gate, kernel, bias, w_out, grad_out):
    n, n_col = lax.axis_size("row"), lax.axis_size("col")
    m = n_col // n
    rows, feats = frames.shape
    depth, chans = w_value.shape
    total, width = rows * n, feats * n_col
    own = chans // n
    r, c = lax.axis_index("row"), lax.axis_index("col")

    wide = frames.astype(jnp.float32)
    sums = eight(jnp.stack([jnp.sum(wide, axis=1), jnp.sum(wide * wide, axis=1)]))
    frames_full, grad_full, sums = exchange(
        n,
        m,
        1,
        [
            Spread(n, m, (rows, feats), True, 2),
            RowGather(n, (rows, feats), True, 1),
            Small(n, n_col, (8, rows), True),
        ],
        (frames, grad_out, sums),
    )
    mean = sums[:, 0].reshape(total) / width
    inv_std = lax.rsqrt(sums[:, 1].reshape(total) / width - mean * mean + epsilon)
    gain_row = lax.dynamic_slice_in_dim(gain, r * depth, depth, 0)
    normed = (
        (frames_full.astype(jnp.float32) - mean[:, None]) * inv_std[:, None] * gain_row[None, :]
    ).astype(jnp.bfloat16)
    value_part = dot(normed, w_value, (1, 0)).astype(jnp.bfloat16)
    gate_part = dot(normed, w_gate, (1, 0)).astype(jnp.bfloat16)
    act_part = dot(grad_full, w_out, (1, 1)).astype(jnp.bfloat16)
    scaled = jnp.stack(
        [
            jnp.sum(w_value.astype(jnp.float32) * gain_row[:, None], axis=0),
            jnp.sum(w_gate.astype(jnp.float32) * gain_row[:, None], axis=0),
        ]
    )
    value_pre, gate_pre, act_grad, scaled = exchange(
        n,
        m,
        2,
        [
            RowFold(n, (total, own), False, 2),
            Fold(n, m, (total, own), False, 2),
            Small(n, n_col, (8, chans), False),
        ],
        (value_part, gate_part, act_part, eight(scaled)),
    )
    scaled = lax.dynamic_slice_in_dim(jnp.sum(scaled, axis=0), r * own, own, 1)
    gate_sig = jax.nn.sigmoid(gate_pre)
    gated = (value_pre * gate_sig).astype(jnp.bfloat16).astype(jnp.float32)
    taps = lax.dynamic_slice_in_dim(kernel, r * own, own, 1)
    own_bias = lax.dynamic_slice_in_dim(bias, r * own, own, 0)
    conv_parts, glu_parts = [], []
    for begin, end in clips(total):
        ahead = padded(gated[begin:end])
        conv = jnp.zeros((end - begin, own), jnp.float32) + own_bias[None, :]
        for k in range(K):
            conv = conv + taps[k][None, :] * ahead[k : k + end - begin]
        conv_parts.append(conv)
    conv_pre = jnp.concatenate(conv_parts, axis=0)
    conv_sig = jax.nn.sigmoid(conv_pre)
    activated = (conv_pre * conv_sig).astype(jnp.bfloat16)
    conv_grad = (
        act_grad.astype(jnp.float32) * conv_sig * (1.0 + conv_pre * (1.0 - conv_sig))
    ).astype(jnp.bfloat16)
    conv_wide = conv_grad.astype(jnp.float32)
    tap_grads = jnp.zeros((K, own), jnp.float32)
    for begin, end in clips(total):
        back = padded(conv_wide[begin:end])
        ahead = padded(gated[begin:end])
        glu = jnp.zeros((end - begin, own), jnp.float32)
        tap_rows = []
        for k in range(K):
            glu = glu + taps[k][None, :] * back[2 * HALF - k : 2 * HALF - k + end - begin]
            tap_rows.append(jnp.sum(conv_wide[begin:end] * ahead[k : k + end - begin], axis=0))
        glu_parts.append(glu)
        tap_grads = tap_grads + jnp.stack(tap_rows)
    glu_grad = jnp.concatenate(glu_parts, axis=0)
    value_grad = (glu_grad * gate_sig).astype(jnp.bfloat16)
    gate_grad = (glu_grad * value_pre * gate_sig * (1.0 - gate_sig)).astype(jnp.bfloat16)
    bias_grad = jnp.sum(conv_wide, axis=0)
    depthwise = jnp.concatenate([tap_grads, bias_grad[None, :]], axis=0)
    value_wide, gate_wide = value_grad.astype(jnp.float32), gate_grad.astype(jnp.float32)
    norm_sums = jnp.stack(
        [
            jnp.sum(value_wide * scaled[0][None, :] + gate_wide * scaled[1][None, :], axis=1),
            jnp.sum(value_wide * value_pre + gate_wide * gate_pre, axis=1),
        ]
    )
    act_full, value_full, gate_full, norm_sums, depthwise = exchange(
        n,
        m,
        3,
        [
            Spread(n, m, (total, own), False, 2),
            RowGather(n, (total, own), False, 2),
            Small(n, n_col, (8, total), True),
            Small(n, n_col, (K + 1, own), False),
        ],
        (activated, value_grad, gate_grad, eight(norm_sums), depthwise),
    )
    norm_sums = jnp.sum(norm_sums, axis=0)[:2]
    depthwise = jnp.transpose(depthwise, (1, 0, 2)).reshape(K + 1, chans)
    out_part = dot(act_full, w_out, (1, 0)).astype(jnp.bfloat16)
    norm_part = (dot(value_full, w_value, (1, 1)) + dot(gate_full, w_gate, (1, 1))).astype(jnp.bfloat16)
    grad_value = dot(normed, value_full, (0, 0))
    grad_gate = dot(normed, gate_full, (0, 0))
    grad_out_weight = dot(act_full, grad_full, (0, 0))
    gain_part = (
        jnp.sum(w_value.astype(jnp.float32) * grad_value + w_gate.astype(jnp.float32) * grad_gate, axis=1) / gain_row
    )
    out_sum, normed_grad, gain_rows = exchange(
        n,
        m,
        4,
        [
            RowFold(n, (rows, feats), True, 1),
            Fold(n, m, (rows, feats), True, 2),
            Small(n, n_col, (8, depth // 8), True),
        ],
        (out_part, norm_part, gain_part.reshape(8, depth // 8)),
    )
    gain_part = gain_rows.reshape(n * depth)
    grad_gain = lax.dynamic_slice_in_dim(gain_part, c * feats, feats, 0)

    encoded = (wide + out_sum).astype(jnp.bfloat16)
    local_mean = lax.dynamic_slice_in_dim(mean, r * rows, rows, 0)
    local_inv = lax.dynamic_slice_in_dim(inv_std, r * rows, rows, 0)
    local_sums = lax.dynamic_slice_in_dim(norm_sums, r * rows, rows, 1) / width
    centred = (wide - local_mean[:, None]) * local_inv[:, None]
    local_gain = lax.dynamic_slice_in_dim(gain, c * feats, feats, 0)
    hat_grad = normed_grad.astype(jnp.float32) * local_gain[None, :]
    input_grad = (
        grad_out.astype(jnp.float32)
        + local_inv[:, None] * (hat_grad - local_sums[0][:, None] - centred * local_sums[1][:, None])
    ).astype(jnp.bfloat16)
    return (
        encoded,
        input_grad,
        grad_value,
        grad_gate,
        depthwise[:K],
        depthwise[K],
        grad_out_weight,
        grad_gain,
    )


def extended(block, sides, width):
    for axis, dim in sides:
        count = lax.axis_size(axis)
        forward = [(i, i + 1) for i in range(count - 1)]
        backward = [(target, source) for source, target in forward]
        low = lax.ppermute(
            lax.slice_in_dim(block, block.shape[dim] - width, None, axis=dim), axis, forward
        )
        high = lax.ppermute(lax.slice_in_dim(block, 0, width, axis=dim), axis, backward)
        block = jnp.concatenate([low, block, high], axis=dim)
    return block


def tap_masks(positions):
    offsets = jnp.arange(K, dtype=jnp.int32) - K // 2
    placed = (positions % LEN)[None, :] + offsets[:, None]
    return ((placed >= 0) & (placed < LEN)).astype(jnp.float32)


def contract_rows(left, right):
    return lax.dot_general(
        left, right, (((0,), (0,)), ((), ())), preferred_element_type=jnp.float32
    )


def contract_cols(left, right):
    return lax.dot_general(
        left, right, (((1,), (1,)), ((), ())), preferred_element_type=jnp.float32
    )


def narrow_shards(frames, gain, w_value, w_gate, kernel, bias, w_out, grad_out):
    row_count = frames.shape[0]
    col_count = frames.shape[1]
    chan_count = w_value.shape[1]
    width = col_count * lax.axis_size("col")
    half_width = K // 2
    row_start = lax.axis_index("row") * row_count
    col_start = lax.axis_index("col") * col_count
    local_gain = lax.dynamic_slice_in_dim(gain, col_start, col_count, 0)
    wide = frames.astype(jnp.float32)
    sum_row, square_sum = lax.psum((jnp.sum(wide, axis=1), jnp.sum(wide * wide, axis=1)), "col")
    mean_row = sum_row / width
    inv_std = lax.rsqrt(square_sum / width - mean_row * mean_row + epsilon)
    centred = (wide - mean_row[:, None]) * inv_std[:, None]
    normed = lax.all_gather(
        (centred * local_gain[None, :]).astype(jnp.bfloat16), "col", axis=1, tiled=True
    )
    value_full, gate_full = (
        lax.all_gather(w_value, "row", axis=0, tiled=True),
        lax.all_gather(w_gate, "row", axis=0, tiled=True),
    )
    value_pre = jnp.dot(normed, value_full, preferred_element_type=jnp.float32)
    gate_pre = jnp.dot(normed, gate_full, preferred_element_type=jnp.float32)
    gate_sig = jax.nn.sigmoid(gate_pre)
    gated = (value_pre * gate_sig).astype(jnp.bfloat16)
    padded_glu = extended(gated, (("row", 0),), half_width).astype(jnp.float32)
    local_masks = tap_masks(row_start + jnp.arange(row_count, dtype=jnp.int32))
    conv_pre = jnp.zeros((row_count, chan_count), jnp.float32) + bias[None, :]
    for tap_index in range(K):
        conv_pre = (
            conv_pre
            + kernel[tap_index][None, :]
            * local_masks[tap_index][:, None]
            * padded_glu[tap_index : tap_index + row_count]
        )
    conv_sig = jax.nn.sigmoid(conv_pre)
    activated = (conv_pre * conv_sig).astype(jnp.bfloat16)
    act_full = lax.all_gather(activated, "col", axis=1, tiled=True)
    out_full = lax.all_gather(w_out, "row", axis=0, tiled=True)
    encoded = (
        frames.astype(jnp.float32) + jnp.dot(act_full, out_full, preferred_element_type=jnp.float32)
    ).astype(jnp.bfloat16)
    act_terms = contract_cols(grad_out, out_full)
    act_grad = lax.psum_scatter(
        act_terms.astype(jnp.bfloat16), "col", scatter_dimension=1, tiled=True
    ).astype(jnp.float32)
    grad_out_weight = lax.psum_scatter(
        contract_rows(act_full, grad_out).astype(jnp.bfloat16),
        "row",
        scatter_dimension=0,
        tiled=True,
    ).astype(jnp.float32)
    conv_grad = (act_grad * conv_sig * (1.0 + conv_pre * (1.0 - conv_sig))).astype(jnp.bfloat16)
    conv_wide = conv_grad.astype(jnp.float32)
    padded_grad = extended(conv_grad, (("row", 0),), half_width).astype(jnp.float32)
    outer_masks = tap_masks(
        row_start - half_width + jnp.arange(row_count + 2 * half_width, dtype=jnp.int32)
    )
    glu_grad = jnp.zeros((row_count, chan_count), jnp.float32)
    kernel_rows = []
    for tap_index in range(K):
        begin = 2 * half_width - tap_index
        glu_grad = (
            glu_grad
            + kernel[tap_index][None, :]
            * outer_masks[tap_index, begin : begin + row_count][:, None]
            * padded_grad[begin : begin + row_count]
        )
        kernel_rows.append(
            jnp.sum(
                local_masks[tap_index][:, None]
                * conv_wide
                * padded_glu[tap_index : tap_index + row_count],
                axis=0,
            )
        )
    kernel_term = jnp.stack(kernel_rows)
    bias_term = jnp.sum(conv_wide, axis=0)
    grad_kernel, grad_bias = lax.psum((kernel_term, bias_term), "row")
    value_grad = (glu_grad * gate_sig).astype(jnp.bfloat16)
    gate_grad = (glu_grad * value_pre * gate_sig * (1.0 - gate_sig)).astype(jnp.bfloat16)
    both_grads = jnp.concatenate([value_grad, gate_grad], axis=1)
    in_weight = lax.psum_scatter(
        contract_rows(normed, both_grads).astype(jnp.bfloat16),
        "row",
        scatter_dimension=0,
        tiled=True,
    ).astype(jnp.float32)
    grad_value = in_weight[:, :chan_count]
    grad_gate = in_weight[:, chan_count:]
    norm_terms = contract_cols(value_grad, value_full) + contract_cols(gate_grad, gate_full)
    normed_grad = lax.psum_scatter(
        norm_terms.astype(jnp.bfloat16), "col", scatter_dimension=1, tiled=True
    ).astype(jnp.float32)
    hat_grad = normed_grad * local_gain[None, :]
    first_sum, second_sum = lax.psum(
        (jnp.sum(hat_grad, axis=1), jnp.sum(hat_grad * centred, axis=1)), "col"
    )
    input_grad = (
        grad_out.astype(jnp.float32)
        + inv_std[:, None]
        * (hat_grad - first_sum[:, None] / width - centred * (second_sum / width)[:, None])
    ).astype(jnp.bfloat16)
    gain_term = jnp.sum(normed_grad * centred, axis=0)
    grad_gain = lax.psum(gain_term, "row")
    return (
        encoded,
        input_grad,
        grad_value,
        grad_gate,
        grad_kernel,
        grad_bias,
        grad_out_weight,
        grad_gain,
    )


def choose(frames, gain, w_value, *others):
    fits = w_value.shape[1] % (128 * lax.axis_size("row")) == 0 and lax.axis_size("col") % lax.axis_size("row") == 0
    return (shards if fits else narrow_shards)(frames, gain, w_value, *others)


def solution(mesh):
    tile = P("row", "col")
    return jax.shard_map(
        choose,
        mesh=mesh,
        in_specs=(tile, P(), tile, tile, P(None, "col"), P("col"), tile, tile),
        out_specs=(tile, tile, tile, tile, P(None, "col"), P("col"), tile, P("col")),
        check_vma=False,
    )
```

```python
import jax
import jax.numpy as jnp
from jax import lax
from jax.experimental import pallas as pl
from jax.experimental.pallas import tpu as pltpu
from jax.sharding import PartitionSpec as P

K = 31
LEN = 2048
HALF = K // 2
epsilon = 1e-05
MESH = pl.DeviceIdType.MESH
ANY = pl.BlockSpec(memory_space=pl.ANY)
VMEM = pl.BlockSpec(memory_space=pltpu.VMEM)
DMA = pltpu.SemaphoreType.DMA


def send(src, dst, sent, arrived, row, col):
    return pltpu.make_async_remote_copy(
        src_ref=src,
        dst_ref=dst,
        send_sem=sent,
        recv_sem=arrived,
        device_id=(row, col),
        device_id_type=MESH,
    )


def await_bytes(ref, sem):
    pltpu.make_async_copy(ref, ref, sem).wait()


def span(index, size):
    if isinstance(index, int):
        return pl.ds(index * size, size)
    return pl.ds(pl.multiple_of(index * size, size), size)


def by_rows(rows, cols, body):
    chunk = max(16, min(rows, 16384 // cols))
    while rows % chunk:
        chunk -= 16

    @pl.loop(0, rows // chunk)
    def _(step):
        body(span(step, chunk))


class Spread:
    def __init__(self, n, m, block, by_frames, cuts):
        self.n, self.m, self.block, self.by_frames, self.cuts = n, m, block, by_frames, cuts
        a, b = block
        whole = (n * a, m * b) if by_frames else (a, n * m * b)
        self.out_shape = [jax.ShapeDtypeStruct(whole, jnp.bfloat16)]
        self.out_specs = [VMEM]
        self.in_specs = [ANY]
        self.scratch = [DMA((n, cuts, m)), DMA((2 + m, n * cuts)), DMA((cuts,))]
        self.phases = n * cuts + 2

    def part(self, ref, k, y, cut):
        a, b = self.block
        high = a // self.cuts
        if self.by_frames:
            return ref.at[span(k * self.cuts + cut, high), span(y, b)]
        return ref.at[span(cut, high), span(y * self.n + k, b)]

    def run(self, phase, refs):
        x, out, arrived, sent, first = refs
        n, m, cuts = self.n, self.m, self.cuts
        r, c = lax.axis_index("row"), lax.axis_index("col")
        z, y = c // m, c % m

        def moves(q):
            k, cut = q // cuts, q % cuts
            mine = self.part(out, k, y, cut)
            came = arrived.at[k, cut, y]

            def up():
                return send(mine, mine, sent.at[0, q], came, r, lax.rem(c + m, n * m))

            def down():
                return send(mine, mine, sent.at[1, q], came, r, lax.rem(c + n * m - m, n * m))

            def side(d):
                return send(mine, mine, sent.at[1 + d, q], came, r, z * m + lax.rem(y + d, m))

            return up, down, side

        def own(cut):
            return x.at[span(cut, self.block[0] // cuts), :]

        def home(cut):
            return send(own(cut), self.part(out, r, y, cut), first.at[cut], arrived.at[r, cut, y], z, c)

        goes_up = jnp.logical_and(z >= r, z < n - 1)
        goes_down = jnp.logical_and(z <= r, z > 0)
        if phase == 0:

            @pl.when(r == z)
            def _():
                for cut in range(cuts):
                    pltpu.make_async_copy(own(cut), self.part(out, r, y, cut), arrived.at[r, cut, y]).start()

            @pl.when(r != z)
            def _():
                for cut in range(cuts):
                    home(cut).start()
        elif phase <= n * cuts:
            q = phase - 1
            await_bytes(self.part(out, q // cuts, y, q % cuts), arrived.at[q // cuts, q % cuts, y])
            up, down, side = moves(q)

            @pl.when(goes_up)
            def _():
                up().start()

            @pl.when(goes_down)
            def _():
                down().start()

            for d in range(1, m):
                side(d).start()
        else:
            for q in range(n * cuts):
                for d in range(1, m):
                    other = lax.rem(y + d, m)
                    await_bytes(self.part(out, q // cuts, other, q % cuts), arrived.at[q // cuts, q % cuts, other])
            for q in range(n * cuts):
                up, down, side = moves(q)

                @pl.when(goes_up)
                def _():
                    up().wait_send()

                @pl.when(goes_down)
                def _():
                    down().wait_send()

                for d in range(1, m):
                    side(d).wait_send()

            @pl.when(r != z)
            def _():
                for cut in range(cuts):
                    home(cut).wait_send()


class Fold:
    window = 6

    def __init__(self, n, m, block, by_frames, cuts):
        self.n, self.m, self.block, self.by_frames, self.cuts = n, m, block, by_frames, cuts
        self.out_shape = [jax.ShapeDtypeStruct(block, jnp.bfloat16)]
        self.out_specs = [VMEM]
        self.in_specs = [VMEM]
        piece = (block[0] // cuts, block[1])
        count = n * cuts
        self.scratch = [
            pltpu.VMEM((count, m) + piece, jnp.bfloat16),
            pltpu.VMEM((2, count) + piece, jnp.bfloat16),
            pltpu.VMEM((count,) + piece, jnp.bfloat16),
            DMA((count, m)),
            DMA((count, m)),
            DMA((2, count)),
            DMA((count,)),
            DMA((cuts,)),
        ]
        self.phases = count + 2

    part = Spread.part

    def run(self, phase, refs):
        parts, out, ybuf, zbuf, sbuf, ysent, ycame, zcame, zsent, ocame = refs
        n, m, cuts = self.n, self.m, self.cuts
        a, b = self.block
        high = a // cuts
        r, c = lax.axis_index("row"), lax.axis_index("col")
        z, y = c // m, c % m
        lower, upper = lax.rem(c + n * m - m, n * m), lax.rem(c + m, n * m)

        def side(q, d):
            other = lax.rem(y + d, m)
            mine = self.part(parts, q // cuts, other, q % cuts)
            return send(mine, ybuf.at[q, y], ysent.at[q, d], ycame.at[q, y], r, z * m + other)

        def onward(q):
            def down():
                return send(sbuf.at[q], zbuf.at[0, q], zsent.at[q], zcame.at[0, q], r, lower)

            def up():
                return send(sbuf.at[q], zbuf.at[1, q], zsent.at[q], zcame.at[1, q], r, upper)

            def home():
                cut = q % cuts
                return send(sbuf.at[q], out.at[span(cut, high), :], zsent.at[q], ocame.at[cut], q // cuts, c)

            return down, up, home

        if phase == 0:
            for q in range(min(self.window, n * cuts)):
                for d in range(1, m):
                    side(q, d).start()
        elif phase <= n * cuts:
            q = phase - 1
            k, cut = q // cuts, q % cuts
            for d in range(1, m):
                other = lax.rem(y + d, m)
                await_bytes(ybuf.at[q, other], ycame.at[q, other])
                side(q, d).wait_send()
                if q + self.window < n * cuts:
                    side(q + self.window, d).start()
            mine = self.part(parts, k, y, cut)

            def add(which):
                for w in which:
                    await_bytes(zbuf.at[w, q], zcame.at[w, q])

                def body(rows):
                    total = mine[rows, :].astype(jnp.float32)
                    for d in range(1, m):
                        total = total + ybuf[q, lax.rem(y + d, m), rows, :].astype(jnp.float32)
                    for w in which:
                        total = total + zbuf[w, q, rows, :].astype(jnp.float32)
                    sbuf[q, rows, :] = total.astype(jnp.bfloat16)

                by_rows(high, b, body)

            above = jnp.logical_and(z >= r, z < n - 1)
            below = jnp.logical_and(z <= r, z > 0)

            @pl.when(jnp.logical_and(above, below))
            def _():
                add((0, 1))

            @pl.when(jnp.logical_and(above, jnp.logical_not(below)))
            def _():
                add((0,))

            @pl.when(jnp.logical_and(jnp.logical_not(above), below))
            def _():
                add((1,))

            @pl.when(jnp.logical_not(jnp.logical_or(above, below)))
            def _():
                add(())

            down, up, home = onward(q)

            @pl.when(z > r)
            def _():
                down().start()

            @pl.when(z < r)
            def _():
                up().start()

            @pl.when(jnp.logical_and(z == r, r != k))
            def _():
                home().start()

            @pl.when(jnp.logical_and(z == r, r == k))
            def _():
                def keep(rows):
                    out.at[span(cut, high), :][rows, :] = sbuf[q, rows, :]

                by_rows(high, b, keep)
        else:

            @pl.when(z != r)
            def _():
                for cut in range(cuts):
                    await_bytes(out.at[span(cut, high), :], ocame.at[cut])

            for q in range(n * cuts):
                down, up, home = onward(q)

                @pl.when(jnp.logical_or(z != r, r != q // cuts))
                def _():
                    down().wait_send()


class Small:
    def __init__(self, n, n_col, block, over_col):
        self.n, self.n_col, self.over_col = n, n_col, over_col
        self.out_shape = [jax.ShapeDtypeStruct((n,) + block, jnp.float32)]
        self.out_specs = [VMEM]
        self.in_specs = [VMEM]
        self.scratch = [
            pltpu.VMEM((n_col,) + block, jnp.float32),
            pltpu.VMEM(block, jnp.float32),
            DMA((n_col,)),
            DMA((n_col,)),
            DMA((n,)),
            DMA((n,)),
        ]
        self.phases = 3

    def run(self, phase, refs):
        x, out, slots, total, csent, ccame, rsent, rcame = refs
        n, n_col = self.n, self.n_col
        r, c = lax.axis_index("row"), lax.axis_index("col")

        def to_col(d):
            return send(x, slots.at[c], csent.at[d], ccame.at[c], r, lax.rem(c + d, n_col))

        def to_row(d):
            return send(total, out.at[r], rsent.at[d], rcame.at[r], lax.rem(r + d, n), c)

        if phase == 0:
            if self.over_col:
                for d in range(1, n_col):
                    to_col(d).start()
        elif phase == 1:
            if self.over_col:
                slots[c] = x[...]
                for d in range(1, n_col):
                    other = lax.rem(c + d, n_col)
                    await_bytes(slots.at[other], ccame.at[other])
                value = slots[0]
                for j in range(1, n_col):
                    value = value + slots[j]
                total[...] = value
            else:
                total[...] = x[...]
            for d in range(1, n):
                to_row(d).start()
            out[r] = total[...]
        else:
            for d in range(1, n):
                other = lax.rem(r + d, n)
                await_bytes(out.at[other], rcame.at[other])
            for d in range(1, n):
                to_row(d).wait_send()
            if self.over_col:
                for d in range(1, n_col):
                    to_col(d).wait_send()


class RowFold:
    def __init__(self, n, block, by_frames, count):
        self.n, self.block, self.by_frames, self.count = n, block, by_frames, count
        half = n // 2
        self.out_shape = [jax.ShapeDtypeStruct(block, jnp.float32)] * count
        self.out_specs = [VMEM] * count
        self.in_specs = [VMEM] * count
        buf = pltpu.VMEM((count, half) + block, jnp.bfloat16)
        sem = DMA((count, half))
        self.scratch = [buf, buf, buf, sem, sem, sem, sem]
        self.phases = 3

    def part(self, ref, k):
        a, b = self.block
        return ref.at[span(k, a), :] if self.by_frames else ref.at[:, span(k, b)]

    def run(self, phase, refs):
        count = self.count
        parts, outs = refs[:count], refs[count : 2 * count]
        near, far, sums, nsent, ncame, fsent, fcame = refs[2 * count :]
        n = self.n
        half = n // 2
        a, b = self.block
        r, c = lax.axis_index("row"), lax.axis_index("col")
        x, core = r // 2, r % 2
        sibling = x * 2 + 1 - core

        def to_sibling(j, d):
            g = lax.rem(x + d, half)
            return send(
                self.part(parts[j], g * 2 + 1 - core), near.at[j, g], nsent.at[j, g], ncame.at[j, g], sibling, c
            )

        def across(j, d):
            g = lax.rem(x + d, half)
            return send(sums.at[j, g], far.at[j, x], fsent.at[j, g], fcame.at[j, x], g * 2 + core, c)

        order = list(range(1, half)) + [0]
        if phase == 0:
            for d in order:
                for j in range(count):
                    to_sibling(j, d).start()
        elif phase == 1:
            for d in range(1, half):
                g = lax.rem(x + d, half)
                for j in range(count):
                    await_bytes(near.at[j, g], ncame.at[j, g])
                    mine = self.part(parts[j], g * 2 + core)

                    def add(rows):
                        sums[j, g, rows, :] = (
                            mine[rows, :].astype(jnp.float32) + near[j, g, rows, :].astype(jnp.float32)
                        ).astype(jnp.bfloat16)

                    by_rows(a, b, add)
                    across(j, d).start()
        else:
            for j in range(count):
                await_bytes(near.at[j, x], ncame.at[j, x])
                for d in range(1, half):
                    g = lax.rem(x + d, half)
                    await_bytes(far.at[j, g], fcame.at[j, g])
                mine = self.part(parts[j], r)

                def total(rows):
                    value = mine[rows, :].astype(jnp.float32) + near[j, x, rows, :].astype(jnp.float32)
                    for d in range(1, half):
                        value = value + far[j, lax.rem(x + d, half), rows, :].astype(jnp.float32)
                    outs[j][rows, :] = value

                by_rows(a, b, total)
            for j in range(count):
                for d in order:
                    to_sibling(j, d).wait_send()
                for d in range(1, half):
                    across(j, d).wait_send()


class RowGather:
    late = True

    def __init__(self, n, block, by_frames, count):
        self.n, self.block, self.by_frames, self.count = n, block, by_frames, count
        a, b = block
        whole = (n * a, b) if by_frames else (a, n * b)
        half = n // 2
        self.out_shape = [jax.ShapeDtypeStruct(whole, jnp.bfloat16)] * count
        self.out_specs = [VMEM] * count
        self.in_specs = [ANY] * count
        self.scratch = [DMA((count, n)), DMA((count, half)), DMA((count, half)), DMA((count,))]
        self.phases = 3

    part = RowFold.part

    def run(self, phase, refs):
        count = self.count
        xs, outs = refs[:count], refs[count : 2 * count]
        came, fsent, nsent, kept = refs[2 * count :]
        n = self.n
        half = n // 2
        r, c = lax.axis_index("row"), lax.axis_index("col")
        x, core = r // 2, r % 2
        sibling = x * 2 + 1 - core

        def keep(j):
            return pltpu.make_async_copy(xs[j], self.part(outs[j], r), kept.at[j])

        def across(j, d):
            g = lax.rem(x + d, half)
            return send(xs[j], self.part(outs[j], r), fsent.at[j, d], came.at[j, r], g * 2 + core, c)

        def to_sibling(j, d):
            g = lax.rem(x + d, half)
            block = self.part(outs[j], g * 2 + core)
            source = xs[j] if d == 0 else block
            return send(source, block, nsent.at[j, d], came.at[j, g * 2 + core], sibling, c)

        if phase == 0:
            for j in range(count):
                for d in range(1, half):
                    across(j, d).start()
                to_sibling(j, 0).start()
                keep(j).start()
        elif phase == 1:
            for d in range(1, half):
                g = lax.rem(x + d, half)
                for j in range(count):
                    await_bytes(self.part(outs[j], g * 2 + core), came.at[j, g * 2 + core])
                    to_sibling(j, d).start()
        else:
            for j in range(count):
                for d in range(half):
                    g = lax.rem(x + d, half)
                    await_bytes(self.part(outs[j], g * 2 + 1 - core), came.at[j, g * 2 + 1 - core])
                keep(j).wait()
                for d in range(1, half):
                    across(j, d).wait_send()
                for d in range(half):
                    to_sibling(j, d).wait_send()


class Products:
    tile = 128

    def __init__(self, n, n_col, frames, depth, chans, steps):
        self.depth, self.chans = depth, chans
        grads = jax.ShapeDtypeStruct((depth, chans), jnp.float32)
        tiles = depth // self.tile
        self.small = Small(n, n_col, (tiles, self.tile), True)
        self.in_specs = [VMEM] + [ANY] * 4 + [VMEM] * 2
        self.out_shape = [grads] * 3 + self.small.out_shape
        self.out_specs = [VMEM] * 3 + self.small.out_specs
        self.scratch = [
            pltpu.VMEM((tiles, self.tile), jnp.float32),
            pltpu.VMEM((frames, depth), jnp.bfloat16),
            pltpu.VMEM((frames, chans), jnp.bfloat16),
            pltpu.VMEM((frames, chans), jnp.bfloat16),
            pltpu.VMEM((frames, chans), jnp.bfloat16),
            DMA((4,)),
        ] + self.small.scratch
        self.phases = steps
        work = [("both", i) for i in range(tiles)] + [("small", 0)]
        work += [("out", i) for i in range(tiles)]
        work.insert(tiles + 3, ("small", 1))
        self.work = {}
        for place, item in enumerate(work):
            self.work.setdefault(1 + place * (steps - 2) // len(work), []).append(item)
        self.work[steps - 1] = [("small", 2)]

    def run(self, phase, refs):
        normed, w_value, w_gate = refs[0], refs[5], refs[6]
        g_value, g_gate, g_out, gain_out = refs[7:11]
        gain_sum, act, grad, value, gate, loaded = refs[11:17]
        tile = self.tile

        def load(j):
            return pltpu.make_async_copy(refs[1 + j], refs[12 + j], loaded.at[j])

        if phase == 0:
            for j in (2, 3, 1, 0):
                load(j).start()
        elif phase == 1:
            for j in range(4):
                load(j).wait()
        for kind, i in self.work.get(phase, []):
            here = pl.ds(i * tile, tile)
            if kind == "small":
                self.small.run(i, (gain_sum, gain_out) + tuple(refs[17:]))
            elif kind == "both":
                left = normed[:, here]
                first = dot(left, value[...], (0, 0))
                g_value[here, :] = first
                total = first * w_value[here, :].astype(jnp.float32)
                second = dot(left, gate[...], (0, 0))
                g_gate[here, :] = second
                total = total + second * w_gate[here, :].astype(jnp.float32)
                narrow = total[:, :tile]
                for j in range(1, self.chans // tile):
                    narrow = narrow + total[:, j * tile : (j + 1) * tile]
                gain_sum[pl.ds(i, 1), :] = jnp.sum(narrow.T, axis=0, keepdims=True)
            else:
                g_out[here, :] = dot(act[:, here], grad[...], (0, 0))


def greet(n, n_col):
    r, c = lax.axis_index("row"), lax.axis_index("col")
    barrier = pltpu.get_barrier_semaphore()

    def hello(row, col):
        pl.semaphore_signal(barrier, inc=1, device_id=(row, col), device_id_type=MESH)

    for d in range(1, n):
        hello(lax.rem(r + d, n), c)
    for d in range(1, n_col):
        hello(r, lax.rem(c + d, n_col))
    pl.semaphore_wait(barrier, n - 1 + n_col - 1)


def exchange(n, m, ident, moves, operands):
    in_specs = [s for mv in moves for s in mv.in_specs]
    out_specs = [s for mv in moves for s in mv.out_specs]
    out_shape = [s for mv in moves for s in mv.out_shape]
    scratch = [s for mv in moves for s in mv.scratch]

    def body(*refs):
        ins = refs[: len(in_specs)]
        outs = refs[len(in_specs) : len(in_specs) + len(out_specs)]
        rest = refs[len(in_specs) + len(out_specs) :]
        own = []
        i = o = s = 0
        for mv in moves:
            own.append(
                tuple(ins[i : i + len(mv.in_specs)])
                + tuple(outs[o : o + len(mv.out_specs)])
                + tuple(rest[s : s + len(mv.scratch)])
            )
            i, o, s = i + len(mv.in_specs), o + len(mv.out_specs), s + len(mv.scratch)
        greet(n, n * m)
        steps = max(mv.phases for mv in moves)
        for step in range(steps):
            for mv, mine in zip(moves, own):
                late = getattr(mv, "late", False) and steps > mv.phases
                at = {0: 0, (steps // 2 if late else 1): 1, steps - 1: 2}
                if mv.phases == steps:
                    mv.run(step, mine)
                elif step in at:
                    mv.run(at[step], mine)

    return pl.pallas_call(
        body,
        out_shape=out_shape,
        in_specs=in_specs,
        out_specs=out_specs,
        scratch_shapes=scratch,
        compiler_params=pltpu.CompilerParams(
            collective_id=ident, has_side_effects=True, vmem_limit_bytes=50 * 2**20
        ),
        cost_estimate=pl.CostEstimate(flops=0, bytes_accessed=100_000_000, transcendentals=0),
    )(*operands)


def dot(left, right, contract):
    return lax.dot_general(left, right, ((contract[:1], contract[1:]), ((), ())), preferred_element_type=jnp.float32)


def eight(block):
    return jnp.pad(block, ((0, 8 - block.shape[0]), (0, 0)))


def clips(total):
    return [(start, min(start + LEN, total)) for start in range(0, total, LEN)]


def padded(block):
    return jnp.pad(block, ((HALF, HALF), (0, 0)))


def shards(frames, gain, w_value, w_gate, kernel, bias, w_out, grad_out):
    n, n_col = lax.axis_size("row"), lax.axis_size("col")
    m = n_col // n
    rows, feats = frames.shape
    depth, chans = w_value.shape
    total, width = rows * n, feats * n_col
    own = chans // n
    r, c = lax.axis_index("row"), lax.axis_index("col")

    wide = frames.astype(jnp.float32)
    sums = eight(jnp.stack([jnp.sum(wide, axis=1), jnp.sum(wide * wide, axis=1)]))
    frames_full, grad_full, sums = exchange(
        n,
        m,
        1,
        [
            Spread(n, m, (rows, feats), True, 4),
            RowGather(n, (rows, feats), True, 1),
            Small(n, n_col, (8, rows), True),
        ],
        (frames, grad_out, sums),
    )
    mean = sums[:, 0].reshape(total) / width
    inv_std = lax.rsqrt(sums[:, 1].reshape(total) / width - mean * mean + epsilon)
    gain_row = lax.dynamic_slice_in_dim(gain, r * depth, depth, 0)
    normed = (
        (frames_full.astype(jnp.float32) - mean[:, None]) * inv_std[:, None] * gain_row[None, :]
    ).astype(jnp.bfloat16)
    value_part = dot(normed, w_value, (1, 0)).astype(jnp.bfloat16)
    gate_part = dot(normed, w_gate, (1, 0)).astype(jnp.bfloat16)
    act_part = dot(grad_full, w_out, (1, 1)).astype(jnp.bfloat16)
    pieces, left = [], gain_row
    for _ in range(3):
        piece = lax.reduce_precision(left, 8, 7)
        pieces.append(piece.astype(jnp.bfloat16))
        left = left - piece
    pieces = eight(jnp.stack(pieces))
    scaled = jnp.stack(
        [jnp.sum(dot(pieces, w_value, (1, 0)), axis=0), jnp.sum(dot(pieces, w_gate, (1, 0)), axis=0)]
    )

    value_pre, gate_pre, act_grad, scaled = exchange(
        n,
        m,
        2,
        [
            RowFold(n, (total, own), False, 2),
            Fold(n, m, (total, own), False, 4),
            Small(n, n_col, (8, chans), False),
        ],
        (value_part, gate_part, act_part, eight(scaled)),
    )
    scaled = lax.dynamic_slice_in_dim(jnp.sum(scaled, axis=0), r * own, own, 1)
    gate_sig = jax.nn.sigmoid(gate_pre)
    gated = (value_pre * gate_sig).astype(jnp.bfloat16).astype(jnp.float32)
    taps = lax.dynamic_slice_in_dim(kernel, r * own, own, 1)
    own_bias = lax.dynamic_slice_in_dim(bias, r * own, own, 0)
    conv_parts, glu_parts = [], []
    for begin, end in clips(total):
        ahead = padded(gated[begin:end])
        conv = jnp.zeros((end - begin, own), jnp.float32) + own_bias[None, :]
        for k in range(K):
            conv = conv + taps[k][None, :] * ahead[k : k + end - begin]
        conv_parts.append(conv)
    conv_pre = jnp.concatenate(conv_parts, axis=0)
    conv_sig = jax.nn.sigmoid(conv_pre)
    activated = (conv_pre * conv_sig).astype(jnp.bfloat16)
    conv_grad = (
        act_grad.astype(jnp.float32) * conv_sig * (1.0 + conv_pre * (1.0 - conv_sig))
    ).astype(jnp.bfloat16)
    conv_wide = conv_grad.astype(jnp.float32)
    tap_grads = jnp.zeros((K, own), jnp.float32)
    for begin, end in clips(total):
        back = padded(conv_wide[begin:end])
        ahead = padded(gated[begin:end])
        glu = jnp.zeros((end - begin, own), jnp.float32)
        tap_rows = []
        for k in range(K):
            glu = glu + taps[k][None, :] * back[2 * HALF - k : 2 * HALF - k + end - begin]
            tap_rows.append(jnp.sum(conv_wide[begin:end] * ahead[k : k + end - begin], axis=0))
        glu_parts.append(glu)
        tap_grads = tap_grads + jnp.stack(tap_rows)
    glu_grad = jnp.concatenate(glu_parts, axis=0)
    value_grad = (glu_grad * gate_sig).astype(jnp.bfloat16)
    gate_grad = (glu_grad * value_pre * gate_sig * (1.0 - gate_sig)).astype(jnp.bfloat16)
    bias_grad = jnp.sum(conv_wide, axis=0)
    depthwise = jnp.concatenate([tap_grads, bias_grad[None, :]], axis=0)
    value_wide, gate_wide = value_grad.astype(jnp.float32), gate_grad.astype(jnp.float32)
    norm_sums = jnp.stack(
        [
            jnp.sum(value_wide * scaled[0][None, :] + gate_wide * scaled[1][None, :], axis=1),
            jnp.sum(value_wide * value_pre + gate_wide * gate_pre, axis=1),
        ]
    )
    act_full, value_full, gate_full, norm_sums, depthwise = exchange(
        n,
        m,
        3,
        [
            Spread(n, m, (total, own), False, 4),
            RowGather(n, (total, own), False, 2),
            Small(n, n_col, (8, total), True),
            Small(n, n_col, (K + 1, own), False),
        ],
        (activated, value_grad, gate_grad, eight(norm_sums), depthwise),
    )
    norm_sums = jnp.sum(norm_sums, axis=0)[:2]
    depthwise = jnp.transpose(depthwise, (1, 0, 2)).reshape(K + 1, chans)
    out_part = dot(act_full, w_out, (1, 0)).astype(jnp.bfloat16)
    norm_part = (dot(value_full, w_value, (1, 1)) + dot(gate_full, w_gate, (1, 1))).astype(jnp.bfloat16)
    fold = Fold(n, m, (rows, feats), True, 4)
    out_sum, normed_grad, grad_value, grad_gate, grad_out_weight, gain_rows = exchange(
        n,
        m,
        4,
        [
            RowFold(n, (rows, feats), True, 1),
            fold,
            Products(n, n_col, total, depth, chans, fold.phases),
        ],
        (out_part, norm_part, normed, act_full, grad_full, value_full, gate_full, w_value, w_gate),
    )
    grad_gain = lax.dynamic_slice_in_dim(gain_rows.reshape(n * depth) / gain, c * feats, feats, 0)

    encoded = (wide + out_sum).astype(jnp.bfloat16)
    local_mean = lax.dynamic_slice_in_dim(mean, r * rows, rows, 0)
    local_inv = lax.dynamic_slice_in_dim(inv_std, r * rows, rows, 0)
    local_sums = lax.dynamic_slice_in_dim(norm_sums, r * rows, rows, 1) / width
    centred = (wide - local_mean[:, None]) * local_inv[:, None]
    local_gain = lax.dynamic_slice_in_dim(gain, c * feats, feats, 0)
    hat_grad = normed_grad.astype(jnp.float32) * local_gain[None, :]
    input_grad = (
        grad_out.astype(jnp.float32)
        + local_inv[:, None] * (hat_grad - local_sums[0][:, None] - centred * local_sums[1][:, None])
    ).astype(jnp.bfloat16)
    return (
        encoded,
        input_grad,
        grad_value,
        grad_gate,
        depthwise[:K],
        depthwise[K],
        grad_out_weight,
        grad_gain,
    )


def extended(block, sides, width):
    for axis, dim in sides:
        count = lax.axis_size(axis)
        forward = [(i, i + 1) for i in range(count - 1)]
        backward = [(target, source) for source, target in forward]
        low = lax.ppermute(
            lax.slice_in_dim(block, block.shape[dim] - width, None, axis=dim), axis, forward
        )
        high = lax.ppermute(lax.slice_in_dim(block, 0, width, axis=dim), axis, backward)
        block = jnp.concatenate([low, block, high], axis=dim)
    return block


def tap_masks(positions):
    offsets = jnp.arange(K, dtype=jnp.int32) - K // 2
    placed = (positions % LEN)[None, :] + offsets[:, None]
    return ((placed >= 0) & (placed < LEN)).astype(jnp.float32)


def contract_rows(left, right):
    return lax.dot_general(
        left, right, (((0,), (0,)), ((), ())), preferred_element_type=jnp.float32
    )


def contract_cols(left, right):
    return lax.dot_general(
        left, right, (((1,), (1,)), ((), ())), preferred_element_type=jnp.float32
    )


def narrow_shards(frames, gain, w_value, w_gate, kernel, bias, w_out, grad_out):
    row_count = frames.shape[0]
    col_count = frames.shape[1]
    chan_count = w_value.shape[1]
    width = col_count * lax.axis_size("col")
    half_width = K // 2
    row_start = lax.axis_index("row") * row_count
    col_start = lax.axis_index("col") * col_count
    local_gain = lax.dynamic_slice_in_dim(gain, col_start, col_count, 0)
    wide = frames.astype(jnp.float32)
    sum_row, square_sum = lax.psum((jnp.sum(wide, axis=1), jnp.sum(wide * wide, axis=1)), "col")
    mean_row = sum_row / width
    inv_std = lax.rsqrt(square_sum / width - mean_row * mean_row + epsilon)
    centred = (wide - mean_row[:, None]) * inv_std[:, None]
    normed = lax.all_gather(
        (centred * local_gain[None, :]).astype(jnp.bfloat16), "col", axis=1, tiled=True
    )
    value_full, gate_full = (
        lax.all_gather(w_value, "row", axis=0, tiled=True),
        lax.all_gather(w_gate, "row", axis=0, tiled=True),
    )
    value_pre = jnp.dot(normed, value_full, preferred_element_type=jnp.float32)
    gate_pre = jnp.dot(normed, gate_full, preferred_element_type=jnp.float32)
    gate_sig = jax.nn.sigmoid(gate_pre)
    gated = (value_pre * gate_sig).astype(jnp.bfloat16)
    padded_glu = extended(gated, (("row", 0),), half_width).astype(jnp.float32)
    local_masks = tap_masks(row_start + jnp.arange(row_count, dtype=jnp.int32))
    conv_pre = jnp.zeros((row_count, chan_count), jnp.float32) + bias[None, :]
    for tap_index in range(K):
        conv_pre = (
            conv_pre
            + kernel[tap_index][None, :]
            * local_masks[tap_index][:, None]
            * padded_glu[tap_index : tap_index + row_count]
        )
    conv_sig = jax.nn.sigmoid(conv_pre)
    activated = (conv_pre * conv_sig).astype(jnp.bfloat16)
    act_full = lax.all_gather(activated, "col", axis=1, tiled=True)
    out_full = lax.all_gather(w_out, "row", axis=0, tiled=True)
    encoded = (
        frames.astype(jnp.float32) + jnp.dot(act_full, out_full, preferred_element_type=jnp.float32)
    ).astype(jnp.bfloat16)
    act_terms = contract_cols(grad_out, out_full)
    act_grad = lax.psum_scatter(
        act_terms.astype(jnp.bfloat16), "col", scatter_dimension=1, tiled=True
    ).astype(jnp.float32)
    grad_out_weight = lax.psum_scatter(
        contract_rows(act_full, grad_out).astype(jnp.bfloat16),
        "row",
        scatter_dimension=0,
        tiled=True,
    ).astype(jnp.float32)
    conv_grad = (act_grad * conv_sig * (1.0 + conv_pre * (1.0 - conv_sig))).astype(jnp.bfloat16)
    conv_wide = conv_grad.astype(jnp.float32)
    padded_grad = extended(conv_grad, (("row", 0),), half_width).astype(jnp.float32)
    outer_masks = tap_masks(
        row_start - half_width + jnp.arange(row_count + 2 * half_width, dtype=jnp.int32)
    )
    glu_grad = jnp.zeros((row_count, chan_count), jnp.float32)
    kernel_rows = []
    for tap_index in range(K):
        begin = 2 * half_width - tap_index
        glu_grad = (
            glu_grad
            + kernel[tap_index][None, :]
            * outer_masks[tap_index, begin : begin + row_count][:, None]
            * padded_grad[begin : begin + row_count]
        )
        kernel_rows.append(
            jnp.sum(
                local_masks[tap_index][:, None]
                * conv_wide
                * padded_glu[tap_index : tap_index + row_count],
                axis=0,
            )
        )
    kernel_term = jnp.stack(kernel_rows)
    bias_term = jnp.sum(conv_wide, axis=0)
    grad_kernel, grad_bias = lax.psum((kernel_term, bias_term), "row")
    value_grad = (glu_grad * gate_sig).astype(jnp.bfloat16)
    gate_grad = (glu_grad * value_pre * gate_sig * (1.0 - gate_sig)).astype(jnp.bfloat16)
    both_grads = jnp.concatenate([value_grad, gate_grad], axis=1)
    in_weight = lax.psum_scatter(
        contract_rows(normed, both_grads).astype(jnp.bfloat16),
        "row",
        scatter_dimension=0,
        tiled=True,
    ).astype(jnp.float32)
    grad_value = in_weight[:, :chan_count]
    grad_gate = in_weight[:, chan_count:]
    norm_terms = contract_cols(value_grad, value_full) + contract_cols(gate_grad, gate_full)
    normed_grad = lax.psum_scatter(
        norm_terms.astype(jnp.bfloat16), "col", scatter_dimension=1, tiled=True
    ).astype(jnp.float32)
    hat_grad = normed_grad * local_gain[None, :]
    first_sum, second_sum = lax.psum(
        (jnp.sum(hat_grad, axis=1), jnp.sum(hat_grad * centred, axis=1)), "col"
    )
    input_grad = (
        grad_out.astype(jnp.float32)
        + inv_std[:, None]
        * (hat_grad - first_sum[:, None] / width - centred * (second_sum / width)[:, None])
    ).astype(jnp.bfloat16)
    gain_term = jnp.sum(normed_grad * centred, axis=0)
    grad_gain = lax.psum(gain_term, "row")
    return (
        encoded,
        input_grad,
        grad_value,
        grad_gate,
        grad_kernel,
        grad_bias,
        grad_out_weight,
        grad_gain,
    )


def choose(frames, gain, w_value, *others):
    fits = w_value.shape[1] % (128 * lax.axis_size("row")) == 0 and lax.axis_size("col") % lax.axis_size("row") == 0
    return (shards if fits else narrow_shards)(frames, gain, w_value, *others)


def solution(mesh):
    tile = P("row", "col")
    return jax.shard_map(
        choose,
        mesh=mesh,
        in_specs=(tile, P(), tile, tile, P(None, "col"), P("col"), tile, tile),
        out_specs=(tile, tile, tile, tile, P(None, "col"), P("col"), tile, P("col")),
        check_vma=False,
    )
```

```python
import jax
import jax.numpy as jnp
from jax import lax
from jax.experimental import pallas as pl
from jax.experimental.pallas import tpu as pltpu
from jax.sharding import PartitionSpec as P

K = 31
LEN = 2048
HALF = K // 2
epsilon = 1e-05
MESH = pl.DeviceIdType.MESH
ANY = pl.BlockSpec(memory_space=pl.ANY)
VMEM = pl.BlockSpec(memory_space=pltpu.VMEM)
DMA = pltpu.SemaphoreType.DMA


def send(src, dst, sent, arrived, row, col):
    return pltpu.make_async_remote_copy(
        src_ref=src,
        dst_ref=dst,
        send_sem=sent,
        recv_sem=arrived,
        device_id=(row, col),
        device_id_type=MESH,
    )


def await_bytes(ref, sem):
    pltpu.make_async_copy(ref, ref, sem).wait()


def span(index, size):
    if isinstance(index, int):
        return pl.ds(index * size, size)
    return pl.ds(pl.multiple_of(index * size, size), size)


def by_rows(rows, cols, body):
    chunk = max(16, min(rows, 16384 // cols))
    while rows % chunk:
        chunk -= 16

    @pl.loop(0, rows // chunk)
    def _(step):
        body(span(step, chunk))


class Spread:
    def __init__(self, n, m, block, by_frames, cuts):
        self.n, self.m, self.block, self.by_frames, self.cuts = n, m, block, by_frames, cuts
        a, b = block
        whole = (n * a, m * b) if by_frames else (a, n * m * b)
        self.out_shape = [jax.ShapeDtypeStruct(whole, jnp.bfloat16)]
        self.out_specs = [VMEM]
        self.in_specs = [ANY]
        self.scratch = [DMA((n, cuts, m)), DMA((2 + m, n * cuts)), DMA((cuts,))]
        self.phases = n * cuts + 2

    def part(self, ref, k, y, cut):
        a, b = self.block
        high = a // self.cuts
        if self.by_frames:
            return ref.at[span(k * self.cuts + cut, high), span(y, b)]
        return ref.at[span(cut, high), span(y * self.n + k, b)]

    def run(self, phase, refs):
        x, out, arrived, sent, first = refs
        n, m, cuts = self.n, self.m, self.cuts
        r, c = lax.axis_index("row"), lax.axis_index("col")
        z, y = c // m, c % m

        def moves(q):
            k, cut = q // cuts, q % cuts
            mine = self.part(out, k, y, cut)
            came = arrived.at[k, cut, y]

            def up():
                return send(mine, mine, sent.at[0, q], came, r, lax.rem(c + m, n * m))

            def down():
                return send(mine, mine, sent.at[1, q], came, r, lax.rem(c + n * m - m, n * m))

            def side(d):
                return send(mine, mine, sent.at[1 + d, q], came, r, z * m + lax.rem(y + d, m))

            return up, down, side

        def own(cut):
            return x.at[span(cut, self.block[0] // cuts), :]

        def home(cut):
            return send(own(cut), self.part(out, r, y, cut), first.at[cut], arrived.at[r, cut, y], z, c)

        goes_up = jnp.logical_and(z >= r, z < n - 1)
        goes_down = jnp.logical_and(z <= r, z > 0)
        if phase == 0:

            @pl.when(r == z)
            def _():
                for cut in range(cuts):
                    pltpu.make_async_copy(own(cut), self.part(out, r, y, cut), arrived.at[r, cut, y]).start()

            @pl.when(r != z)
            def _():
                for cut in range(cuts):
                    home(cut).start()
        elif phase <= n * cuts:
            q = phase - 1
            await_bytes(self.part(out, q // cuts, y, q % cuts), arrived.at[q // cuts, q % cuts, y])
            up, down, side = moves(q)

            @pl.when(goes_up)
            def _():
                up().start()

            @pl.when(goes_down)
            def _():
                down().start()

            for d in range(1, m):
                side(d).start()
        else:
            for q in range(n * cuts):
                for d in range(1, m):
                    other = lax.rem(y + d, m)
                    await_bytes(self.part(out, q // cuts, other, q % cuts), arrived.at[q // cuts, q % cuts, other])
            for q in range(n * cuts):
                up, down, side = moves(q)

                @pl.when(goes_up)
                def _():
                    up().wait_send()

                @pl.when(goes_down)
                def _():
                    down().wait_send()

                for d in range(1, m):
                    side(d).wait_send()

            @pl.when(r != z)
            def _():
                for cut in range(cuts):
                    home(cut).wait_send()


class Fold:
    window = 6

    def __init__(self, n, m, block, by_frames, cuts):
        self.n, self.m, self.block, self.by_frames, self.cuts = n, m, block, by_frames, cuts
        self.out_shape = [jax.ShapeDtypeStruct(block, jnp.bfloat16)]
        self.out_specs = [VMEM]
        self.in_specs = [VMEM]
        piece = (block[0] // cuts, block[1])
        count = n * cuts
        self.scratch = [
            pltpu.VMEM((count, m) + piece, jnp.bfloat16),
            pltpu.VMEM((2, count) + piece, jnp.bfloat16),
            pltpu.VMEM((count,) + piece, jnp.bfloat16),
            DMA((count, m)),
            DMA((count, m)),
            DMA((2, count)),
            DMA((count,)),
            DMA((cuts,)),
        ]
        self.phases = count + 2

    part = Spread.part

    def run(self, phase, refs):
        parts, out, ybuf, zbuf, sbuf, ysent, ycame, zcame, zsent, ocame = refs
        n, m, cuts = self.n, self.m, self.cuts
        a, b = self.block
        high = a // cuts
        r, c = lax.axis_index("row"), lax.axis_index("col")
        z, y = c // m, c % m
        lower, upper = lax.rem(c + n * m - m, n * m), lax.rem(c + m, n * m)

        def side(q, d):
            other = lax.rem(y + d, m)
            mine = self.part(parts, q // cuts, other, q % cuts)
            return send(mine, ybuf.at[q, y], ysent.at[q, d], ycame.at[q, y], r, z * m + other)

        def onward(q):
            def down():
                return send(sbuf.at[q], zbuf.at[0, q], zsent.at[q], zcame.at[0, q], r, lower)

            def up():
                return send(sbuf.at[q], zbuf.at[1, q], zsent.at[q], zcame.at[1, q], r, upper)

            def home():
                cut = q % cuts
                return send(sbuf.at[q], out.at[span(cut, high), :], zsent.at[q], ocame.at[cut], q // cuts, c)

            return down, up, home

        if phase == 0:
            for q in range(min(self.window, n * cuts)):
                for d in range(1, m):
                    side(q, d).start()
        elif phase <= n * cuts:
            q = phase - 1
            k, cut = q // cuts, q % cuts
            for d in range(1, m):
                other = lax.rem(y + d, m)
                await_bytes(ybuf.at[q, other], ycame.at[q, other])
                side(q, d).wait_send()
                if q + self.window < n * cuts:
                    side(q + self.window, d).start()
            mine = self.part(parts, k, y, cut)

            def add(which):
                for w in which:
                    await_bytes(zbuf.at[w, q], zcame.at[w, q])

                def body(rows):
                    total = mine[rows, :].astype(jnp.float32)
                    for d in range(1, m):
                        total = total + ybuf[q, lax.rem(y + d, m), rows, :].astype(jnp.float32)
                    for w in which:
                        total = total + zbuf[w, q, rows, :].astype(jnp.float32)
                    sbuf[q, rows, :] = total.astype(jnp.bfloat16)

                by_rows(high, b, body)

            above = jnp.logical_and(z >= r, z < n - 1)
            below = jnp.logical_and(z <= r, z > 0)

            @pl.when(jnp.logical_and(above, below))
            def _():
                add((0, 1))

            @pl.when(jnp.logical_and(above, jnp.logical_not(below)))
            def _():
                add((0,))

            @pl.when(jnp.logical_and(jnp.logical_not(above), below))
            def _():
                add((1,))

            @pl.when(jnp.logical_not(jnp.logical_or(above, below)))
            def _():
                add(())

            down, up, home = onward(q)

            @pl.when(z > r)
            def _():
                down().start()

            @pl.when(z < r)
            def _():
                up().start()

            @pl.when(jnp.logical_and(z == r, r != k))
            def _():
                home().start()

            @pl.when(jnp.logical_and(z == r, r == k))
            def _():
                def keep(rows):
                    out.at[span(cut, high), :][rows, :] = sbuf[q, rows, :]

                by_rows(high, b, keep)
        else:

            @pl.when(z != r)
            def _():
                for cut in range(cuts):
                    await_bytes(out.at[span(cut, high), :], ocame.at[cut])

            for q in range(n * cuts):
                down, up, home = onward(q)

                @pl.when(jnp.logical_or(z != r, r != q // cuts))
                def _():
                    down().wait_send()


class Small:
    def __init__(self, n, n_col, block, over_col):
        self.n, self.n_col, self.over_col = n, n_col, over_col
        self.out_shape = [jax.ShapeDtypeStruct((n,) + block, jnp.float32)]
        self.out_specs = [VMEM]
        self.in_specs = [VMEM]
        self.scratch = [
            pltpu.VMEM((n_col,) + block, jnp.float32),
            pltpu.VMEM(block, jnp.float32),
            DMA((n_col,)),
            DMA((n_col,)),
            DMA((n,)),
            DMA((n,)),
        ]
        self.phases = 3

    def run(self, phase, refs):
        x, out, slots, total, csent, ccame, rsent, rcame = refs
        n, n_col = self.n, self.n_col
        r, c = lax.axis_index("row"), lax.axis_index("col")

        def to_col(d):
            return send(x, slots.at[c], csent.at[d], ccame.at[c], r, lax.rem(c + d, n_col))

        def to_row(d):
            return send(total, out.at[r], rsent.at[d], rcame.at[r], lax.rem(r + d, n), c)

        if phase == 0:
            if self.over_col:
                for d in range(1, n_col):
                    to_col(d).start()
        elif phase == 1:
            if self.over_col:
                slots[c] = x[...]
                for d in range(1, n_col):
                    other = lax.rem(c + d, n_col)
                    await_bytes(slots.at[other], ccame.at[other])
                value = slots[0]
                for j in range(1, n_col):
                    value = value + slots[j]
                total[...] = value
            else:
                total[...] = x[...]
            for d in range(1, n):
                to_row(d).start()
            out[r] = total[...]
        else:
            for d in range(1, n):
                other = lax.rem(r + d, n)
                await_bytes(out.at[other], rcame.at[other])
            for d in range(1, n):
                to_row(d).wait_send()
            if self.over_col:
                for d in range(1, n_col):
                    to_col(d).wait_send()


class RowFold:
    def __init__(self, n, block, by_frames, count):
        self.n, self.block, self.by_frames, self.count = n, block, by_frames, count
        half = n // 2
        self.out_shape = [jax.ShapeDtypeStruct(block, jnp.float32)] * count
        self.out_specs = [VMEM] * count
        self.in_specs = [VMEM] * count
        buf = pltpu.VMEM((count, half) + block, jnp.bfloat16)
        sem = DMA((count, half))
        self.scratch = [buf, buf, buf, sem, sem, sem, sem]
        self.phases = 3

    def part(self, ref, k):
        a, b = self.block
        return ref.at[span(k, a), :] if self.by_frames else ref.at[:, span(k, b)]

    def run(self, phase, refs):
        count = self.count
        parts, outs = refs[:count], refs[count : 2 * count]
        near, far, sums, nsent, ncame, fsent, fcame = refs[2 * count :]
        n = self.n
        half = n // 2
        a, b = self.block
        r, c = lax.axis_index("row"), lax.axis_index("col")
        x, core = r // 2, r % 2
        sibling = x * 2 + 1 - core

        def to_sibling(j, d):
            g = lax.rem(x + d, half)
            return send(
                self.part(parts[j], g * 2 + 1 - core), near.at[j, g], nsent.at[j, g], ncame.at[j, g], sibling, c
            )

        def across(j, d):
            g = lax.rem(x + d, half)
            return send(sums.at[j, g], far.at[j, x], fsent.at[j, g], fcame.at[j, x], g * 2 + core, c)

        order = list(range(1, half)) + [0]
        if phase == 0:
            for d in order:
                for j in range(count):
                    to_sibling(j, d).start()
        elif phase == 1:
            for d in range(1, half):
                g = lax.rem(x + d, half)
                for j in range(count):
                    await_bytes(near.at[j, g], ncame.at[j, g])
                    mine = self.part(parts[j], g * 2 + core)

                    def add(rows):
                        sums[j, g, rows, :] = (
                            mine[rows, :].astype(jnp.float32) + near[j, g, rows, :].astype(jnp.float32)
                        ).astype(jnp.bfloat16)

                    by_rows(a, b, add)
                    across(j, d).start()
        else:
            for j in range(count):
                await_bytes(near.at[j, x], ncame.at[j, x])
                for d in range(1, half):
                    g = lax.rem(x + d, half)
                    await_bytes(far.at[j, g], fcame.at[j, g])
                mine = self.part(parts[j], r)

                def total(rows):
                    value = mine[rows, :].astype(jnp.float32) + near[j, x, rows, :].astype(jnp.float32)
                    for d in range(1, half):
                        value = value + far[j, lax.rem(x + d, half), rows, :].astype(jnp.float32)
                    outs[j][rows, :] = value

                by_rows(a, b, total)
            for j in range(count):
                for d in order:
                    to_sibling(j, d).wait_send()
                for d in range(1, half):
                    across(j, d).wait_send()


class RowGather:
    late = True

    def __init__(self, n, block, by_frames, count):
        self.n, self.block, self.by_frames, self.count = n, block, by_frames, count
        a, b = block
        whole = (n * a, b) if by_frames else (a, n * b)
        half = n // 2
        self.out_shape = [jax.ShapeDtypeStruct(whole, jnp.bfloat16)] * count
        self.out_specs = [VMEM] * count
        self.in_specs = [ANY] * count
        self.scratch = [DMA((count, n)), DMA((count, half)), DMA((count, half)), DMA((count,))]
        self.phases = 3

    part = RowFold.part

    def run(self, phase, refs):
        count = self.count
        xs, outs = refs[:count], refs[count : 2 * count]
        came, fsent, nsent, kept = refs[2 * count :]
        n = self.n
        half = n // 2
        r, c = lax.axis_index("row"), lax.axis_index("col")
        x, core = r // 2, r % 2
        sibling = x * 2 + 1 - core

        def keep(j):
            return pltpu.make_async_copy(xs[j], self.part(outs[j], r), kept.at[j])

        def across(j, d):
            g = lax.rem(x + d, half)
            return send(xs[j], self.part(outs[j], r), fsent.at[j, d], came.at[j, r], g * 2 + core, c)

        def to_sibling(j, d):
            g = lax.rem(x + d, half)
            block = self.part(outs[j], g * 2 + core)
            source = xs[j] if d == 0 else block
            return send(source, block, nsent.at[j, d], came.at[j, g * 2 + core], sibling, c)

        if phase == 0:
            for j in range(count):
                for d in range(1, half):
                    across(j, d).start()
                to_sibling(j, 0).start()
                keep(j).start()
        elif phase == 1:
            for d in range(1, half):
                g = lax.rem(x + d, half)
                for j in range(count):
                    await_bytes(self.part(outs[j], g * 2 + core), came.at[j, g * 2 + core])
                    to_sibling(j, d).start()
        else:
            for j in range(count):
                for d in range(half):
                    g = lax.rem(x + d, half)
                    await_bytes(self.part(outs[j], g * 2 + 1 - core), came.at[j, g * 2 + 1 - core])
                keep(j).wait()
                for d in range(1, half):
                    across(j, d).wait_send()
                for d in range(half):
                    to_sibling(j, d).wait_send()


class Products:
    tile = 128

    def __init__(self, n, n_col, frames, depth, chans, steps):
        self.depth, self.chans = depth, chans
        grads = jax.ShapeDtypeStruct((depth, chans), jnp.float32)
        tiles = depth // self.tile
        self.small = Small(n, n_col, (tiles, self.tile), True)
        self.in_specs = [VMEM] + [ANY] * 4 + [VMEM] * 2
        self.out_shape = [grads] * 3 + self.small.out_shape
        self.out_specs = [VMEM] * 3 + self.small.out_specs
        self.scratch = [
            pltpu.VMEM((tiles, self.tile), jnp.float32),
            pltpu.VMEM((frames, depth), jnp.bfloat16),
            pltpu.VMEM((frames, chans), jnp.bfloat16),
            pltpu.VMEM((frames, chans), jnp.bfloat16),
            pltpu.VMEM((frames, chans), jnp.bfloat16),
            DMA((4,)),
        ] + self.small.scratch
        self.phases = steps
        work = [("both", i) for i in range(tiles)] + [("small", 0)]
        work += [("out", i) for i in range(tiles)]
        work.insert(tiles + 3, ("small", 1))
        self.work = {}
        for place, item in enumerate(work):
            self.work.setdefault(1 + place * (steps - 2) // len(work), []).append(item)
        self.work[steps - 1] = [("small", 2)]

    def run(self, phase, refs):
        normed, w_value, w_gate = refs[0], refs[5], refs[6]
        g_value, g_gate, g_out, gain_out = refs[7:11]
        gain_sum, act, grad, value, gate, loaded = refs[11:17]
        tile = self.tile

        def load(j):
            return pltpu.make_async_copy(refs[1 + j], refs[12 + j], loaded.at[j])

        if phase == 0:
            for j in (2, 3, 1, 0):
                load(j).start()
        elif phase == 1:
            for j in range(4):
                load(j).wait()
        for kind, i in self.work.get(phase, []):
            here = pl.ds(i * tile, tile)
            if kind == "small":
                self.small.run(i, (gain_sum, gain_out) + tuple(refs[17:]))
            elif kind == "both":
                left = normed[:, here]
                first = dot(left, value[...], (0, 0))
                g_value[here, :] = first
                total = first * w_value[here, :].astype(jnp.float32)
                second = dot(left, gate[...], (0, 0))
                g_gate[here, :] = second
                total = total + second * w_gate[here, :].astype(jnp.float32)
                narrow = total[:, :tile]
                for j in range(1, self.chans // tile):
                    narrow = narrow + total[:, j * tile : (j + 1) * tile]
                gain_sum[pl.ds(i, 1), :] = jnp.sum(narrow.T, axis=0, keepdims=True)
            else:
                g_out[here, :] = dot(act[:, here], grad[...], (0, 0))


def greet(n, n_col):
    r, c = lax.axis_index("row"), lax.axis_index("col")
    barrier = pltpu.get_barrier_semaphore()

    def hello(row, col):
        pl.semaphore_signal(barrier, inc=1, device_id=(row, col), device_id_type=MESH)

    for d in range(1, n):
        hello(lax.rem(r + d, n), c)
    for d in range(1, n_col):
        hello(r, lax.rem(c + d, n_col))
    pl.semaphore_wait(barrier, n - 1 + n_col - 1)


def exchange(n, m, ident, moves, operands):
    in_specs = [s for mv in moves for s in mv.in_specs]
    out_specs = [s for mv in moves for s in mv.out_specs]
    out_shape = [s for mv in moves for s in mv.out_shape]
    scratch = [s for mv in moves for s in mv.scratch]

    def body(*refs):
        ins = refs[: len(in_specs)]
        outs = refs[len(in_specs) : len(in_specs) + len(out_specs)]
        rest = refs[len(in_specs) + len(out_specs) :]
        own = []
        i = o = s = 0
        for mv in moves:
            own.append(
                tuple(ins[i : i + len(mv.in_specs)])
                + tuple(outs[o : o + len(mv.out_specs)])
                + tuple(rest[s : s + len(mv.scratch)])
            )
            i, o, s = i + len(mv.in_specs), o + len(mv.out_specs), s + len(mv.scratch)
        greet(n, n * m)
        steps = max(mv.phases for mv in moves)
        for step in range(steps):
            for mv, mine in zip(moves, own):
                late = getattr(mv, "late", False) and steps > mv.phases
                at = {0: 0, (steps // 2 if late else 1): 1, steps - 1: 2}
                if mv.phases == steps:
                    mv.run(step, mine)
                elif step in at:
                    mv.run(at[step], mine)

    return pl.pallas_call(
        body,
        out_shape=out_shape,
        in_specs=in_specs,
        out_specs=out_specs,
        scratch_shapes=scratch,
        compiler_params=pltpu.CompilerParams(
            collective_id=ident, has_side_effects=True, vmem_limit_bytes=50 * 2**20
        ),
        cost_estimate=pl.CostEstimate(flops=0, bytes_accessed=100_000_000, transcendentals=0),
    )(*operands)


def dot(left, right, contract):
    return lax.dot_general(left, right, ((contract[:1], contract[1:]), ((), ())), preferred_element_type=jnp.float32)


def eight(block):
    return jnp.pad(block, ((0, 8 - block.shape[0]), (0, 0)))


def clips(total):
    return [(start, min(start + LEN, total)) for start in range(0, total, LEN)]


def sigmoid(value):
    return 1.0 / (1.0 + jnp.exp(-value))


def conv_body(bounds, value, gate, act_grad, taps, bias, act, v_grad, g_grad, tap_grads, ahead, back):
    high, edge = 32, 16
    wide = value.shape[1]
    blank = jnp.zeros((edge, wide), jnp.float32)
    tap_grads[...] = jnp.zeros_like(tap_grads)
    for begin, end in bounds:
        length = end - begin
        for buffer in (ahead, back):
            buffer[pl.ds(0, edge), :] = blank
            buffer[pl.ds(edge + length, edge), :] = blank

        @pl.loop(0, length // high)
        def _(i):
            rows = pl.ds(pl.multiple_of(begin + i * high, high), high)
            inner = pl.ds(pl.multiple_of(edge + i * high, edge), high)
            gated = value[rows, :] * sigmoid(gate[rows, :])
            ahead[inner, :] = gated.astype(jnp.bfloat16).astype(jnp.float32)

        @pl.loop(0, length // high)
        def _(i):
            start = pl.multiple_of(i * high, high)
            rows = pl.ds(pl.multiple_of(begin + i * high, high), high)
            inner = pl.ds(pl.multiple_of(edge + i * high, edge), high)
            conv = jnp.broadcast_to(bias[pl.ds(0, 1), :], (high, wide))
            for k in range(K):
                conv = conv + taps[pl.ds(k, 1), :] * ahead[pl.ds(start + (edge - HALF + k), high), :]
            sig = sigmoid(conv)
            act[rows, :] = (conv * sig).astype(jnp.bfloat16)
            grad = act_grad[rows, :].astype(jnp.float32) * sig * (1.0 + conv * (1.0 - sig))
            back[inner, :] = grad.astype(jnp.bfloat16).astype(jnp.float32)

        @pl.loop(0, length // high)
        def _(i):
            start = pl.multiple_of(i * high, high)
            rows = pl.ds(pl.multiple_of(begin + i * high, high), high)
            glu = jnp.zeros((high, wide), jnp.float32)
            for k in range(K):
                glu = glu + taps[pl.ds(k, 1), :] * back[pl.ds(start + (edge + HALF - k), high), :]
            sig = sigmoid(gate[rows, :])
            v_grad[rows, :] = (glu * sig).astype(jnp.bfloat16)
            g_grad[rows, :] = (glu * value[rows, :] * sig * (1.0 - sig)).astype(jnp.bfloat16)
            own = back[pl.ds(pl.multiple_of(edge + i * high, edge), high), :]

            def eights(block):
                part = block[:8]
                for j in range(1, high // 8):
                    part = part + block[8 * j : 8 * j + 8]
                return part

            for k in range(K):
                term = own * ahead[pl.ds(start + (edge - HALF + k), high), :]
                tap_grads[k] = tap_grads[k] + eights(term)
            tap_grads[K] = tap_grads[K] + eights(own)


def conv_stage(value_pre, gate_pre, act_grad, taps, bias):
    total, own = value_pre.shape
    bounds = clips(total)
    longest = max(end - begin for begin, end in bounds)
    half = jax.ShapeDtypeStruct((total, own), jnp.bfloat16)
    return pl.pallas_call(
        lambda *refs: conv_body(bounds, *refs),
        out_shape=[half, half, half, jax.ShapeDtypeStruct((K + 1, 8, own), jnp.float32)],
        in_specs=[VMEM] * 5,
        out_specs=[VMEM] * 4,
        scratch_shapes=[pltpu.VMEM((longest + 32, own), jnp.float32)] * 2,
        compiler_params=pltpu.CompilerParams(vmem_limit_bytes=32 * 2**20),
        cost_estimate=pl.CostEstimate(flops=6 * K * total * own, bytes_accessed=4_000_000, transcendentals=0),
    )(value_pre, gate_pre, act_grad, taps, bias)


def shards(frames, gain, w_value, w_gate, kernel, bias, w_out, grad_out):
    n, n_col = lax.axis_size("row"), lax.axis_size("col")
    m = n_col // n
    rows, feats = frames.shape
    depth, chans = w_value.shape
    total, width = rows * n, feats * n_col
    own = chans // n
    r, c = lax.axis_index("row"), lax.axis_index("col")

    wide = frames.astype(jnp.float32)
    sums = eight(jnp.stack([jnp.sum(wide, axis=1), jnp.sum(wide * wide, axis=1)]))
    frames_full, grad_full, sums = exchange(
        n,
        m,
        1,
        [
            Spread(n, m, (rows, feats), True, 4),
            RowGather(n, (rows, feats), True, 1),
            Small(n, n_col, (8, rows), True),
        ],
        (frames, grad_out, sums),
    )
    mean = sums[:, 0].reshape(total) / width
    inv_std = lax.rsqrt(sums[:, 1].reshape(total) / width - mean * mean + epsilon)
    gain_row = lax.dynamic_slice_in_dim(gain, r * depth, depth, 0)
    normed = (
        (frames_full.astype(jnp.float32) - mean[:, None]) * inv_std[:, None] * gain_row[None, :]
    ).astype(jnp.bfloat16)
    value_part = dot(normed, w_value, (1, 0)).astype(jnp.bfloat16)
    gate_part = dot(normed, w_gate, (1, 0)).astype(jnp.bfloat16)
    act_part = dot(grad_full, w_out, (1, 1)).astype(jnp.bfloat16)
    pieces, left = [], gain_row
    for _ in range(3):
        piece = lax.reduce_precision(left, 8, 7)
        pieces.append(piece.astype(jnp.bfloat16))
        left = left - piece
    pieces = eight(jnp.stack(pieces))
    scaled = jnp.stack(
        [jnp.sum(dot(pieces, w_value, (1, 0)), axis=0), jnp.sum(dot(pieces, w_gate, (1, 0)), axis=0)]
    )

    value_pre, gate_pre, act_grad, scaled = exchange(
        n,
        m,
        2,
        [
            RowFold(n, (total, own), False, 2),
            Fold(n, m, (total, own), False, 4),
            Small(n, n_col, (8, chans), False),
        ],
        (value_part, gate_part, act_part, eight(scaled)),
    )
    scaled = lax.dynamic_slice_in_dim(jnp.sum(scaled, axis=0), r * own, own, 1)
    taps = jnp.pad(lax.dynamic_slice_in_dim(kernel, r * own, own, 1), ((0, 1), (0, 0)))
    own_bias = eight(lax.dynamic_slice_in_dim(bias, r * own, own, 0)[None, :])
    activated, value_grad, gate_grad, tap_grads = conv_stage(value_pre, gate_pre, act_grad, taps, own_bias)
    depthwise = jnp.sum(tap_grads, axis=1)
    value_wide, gate_wide = value_grad.astype(jnp.float32), gate_grad.astype(jnp.float32)
    norm_sums = jnp.stack(
        [
            jnp.sum(value_wide * scaled[0][None, :] + gate_wide * scaled[1][None, :], axis=1),
            jnp.sum(value_wide * value_pre + gate_wide * gate_pre, axis=1),
        ]
    )
    act_full, value_full, gate_full, norm_sums, depthwise = exchange(
        n,
        m,
        3,
        [
            Spread(n, m, (total, own), False, 4),
            RowGather(n, (total, own), False, 2),
            Small(n, n_col, (8, total), True),
            Small(n, n_col, (K + 1, own), False),
        ],
        (activated, value_grad, gate_grad, eight(norm_sums), depthwise),
    )
    norm_sums = jnp.sum(norm_sums, axis=0)[:2]
    depthwise = jnp.transpose(depthwise, (1, 0, 2)).reshape(K + 1, chans)
    out_part = dot(act_full, w_out, (1, 0)).astype(jnp.bfloat16)
    norm_part = (dot(value_full, w_value, (1, 1)) + dot(gate_full, w_gate, (1, 1))).astype(jnp.bfloat16)
    fold = Fold(n, m, (rows, feats), True, 4)
    out_sum, normed_grad, grad_value, grad_gate, grad_out_weight, gain_rows = exchange(
        n,
        m,
        4,
        [
            RowFold(n, (rows, feats), True, 1),
            fold,
            Products(n, n_col, total, depth, chans, fold.phases),
        ],
        (out_part, norm_part, normed, act_full, grad_full, value_full, gate_full, w_value, w_gate),
    )
    grad_gain = lax.dynamic_slice_in_dim(gain_rows.reshape(n * depth) / gain, c * feats, feats, 0)

    encoded = (wide + out_sum).astype(jnp.bfloat16)
    local_mean = lax.dynamic_slice_in_dim(mean, r * rows, rows, 0)
    local_inv = lax.dynamic_slice_in_dim(inv_std, r * rows, rows, 0)
    local_sums = lax.dynamic_slice_in_dim(norm_sums, r * rows, rows, 1) / width
    centred = (wide - local_mean[:, None]) * local_inv[:, None]
    local_gain = lax.dynamic_slice_in_dim(gain, c * feats, feats, 0)
    hat_grad = normed_grad.astype(jnp.float32) * local_gain[None, :]
    input_grad = (
        grad_out.astype(jnp.float32)
        + local_inv[:, None] * (hat_grad - local_sums[0][:, None] - centred * local_sums[1][:, None])
    ).astype(jnp.bfloat16)
    return (
        encoded,
        input_grad,
        grad_value,
        grad_gate,
        depthwise[:K],
        depthwise[K],
        grad_out_weight,
        grad_gain,
    )


def extended(block, sides, width):
    for axis, dim in sides:
        count = lax.axis_size(axis)
        forward = [(i, i + 1) for i in range(count - 1)]
        backward = [(target, source) for source, target in forward]
        low = lax.ppermute(
            lax.slice_in_dim(block, block.shape[dim] - width, None, axis=dim), axis, forward
        )
        high = lax.ppermute(lax.slice_in_dim(block, 0, width, axis=dim), axis, backward)
        block = jnp.concatenate([low, block, high], axis=dim)
    return block


def tap_masks(positions):
    offsets = jnp.arange(K, dtype=jnp.int32) - K // 2
    placed = (positions % LEN)[None, :] + offsets[:, None]
    return ((placed >= 0) & (placed < LEN)).astype(jnp.float32)


def contract_rows(left, right):
    return lax.dot_general(
        left, right, (((0,), (0,)), ((), ())), preferred_element_type=jnp.float32
    )


def contract_cols(left, right):
    return lax.dot_general(
        left, right, (((1,), (1,)), ((), ())), preferred_element_type=jnp.float32
    )


def narrow_shards(frames, gain, w_value, w_gate, kernel, bias, w_out, grad_out):
    row_count = frames.shape[0]
    col_count = frames.shape[1]
    chan_count = w_value.shape[1]
    width = col_count * lax.axis_size("col")
    half_width = K // 2
    row_start = lax.axis_index("row") * row_count
    col_start = lax.axis_index("col") * col_count
    local_gain = lax.dynamic_slice_in_dim(gain, col_start, col_count, 0)
    wide = frames.astype(jnp.float32)
    sum_row, square_sum = lax.psum((jnp.sum(wide, axis=1), jnp.sum(wide * wide, axis=1)), "col")
    mean_row = sum_row / width
    inv_std = lax.rsqrt(square_sum / width - mean_row * mean_row + epsilon)
    centred = (wide - mean_row[:, None]) * inv_std[:, None]
    normed = lax.all_gather(
        (centred * local_gain[None, :]).astype(jnp.bfloat16), "col", axis=1, tiled=True
    )
    value_full, gate_full = (
        lax.all_gather(w_value, "row", axis=0, tiled=True),
        lax.all_gather(w_gate, "row", axis=0, tiled=True),
    )
    value_pre = jnp.dot(normed, value_full, preferred_element_type=jnp.float32)
    gate_pre = jnp.dot(normed, gate_full, preferred_element_type=jnp.float32)
    gate_sig = jax.nn.sigmoid(gate_pre)
    gated = (value_pre * gate_sig).astype(jnp.bfloat16)
    padded_glu = extended(gated, (("row", 0),), half_width).astype(jnp.float32)
    local_masks = tap_masks(row_start + jnp.arange(row_count, dtype=jnp.int32))
    conv_pre = jnp.zeros((row_count, chan_count), jnp.float32) + bias[None, :]
    for tap_index in range(K):
        conv_pre = (
            conv_pre
            + kernel[tap_index][None, :]
            * local_masks[tap_index][:, None]
            * padded_glu[tap_index : tap_index + row_count]
        )
    conv_sig = jax.nn.sigmoid(conv_pre)
    activated = (conv_pre * conv_sig).astype(jnp.bfloat16)
    act_full = lax.all_gather(activated, "col", axis=1, tiled=True)
    out_full = lax.all_gather(w_out, "row", axis=0, tiled=True)
    encoded = (
        frames.astype(jnp.float32) + jnp.dot(act_full, out_full, preferred_element_type=jnp.float32)
    ).astype(jnp.bfloat16)
    act_terms = contract_cols(grad_out, out_full)
    act_grad = lax.psum_scatter(
        act_terms.astype(jnp.bfloat16), "col", scatter_dimension=1, tiled=True
    ).astype(jnp.float32)
    grad_out_weight = lax.psum_scatter(
        contract_rows(act_full, grad_out).astype(jnp.bfloat16),
        "row",
        scatter_dimension=0,
        tiled=True,
    ).astype(jnp.float32)
    conv_grad = (act_grad * conv_sig * (1.0 + conv_pre * (1.0 - conv_sig))).astype(jnp.bfloat16)
    conv_wide = conv_grad.astype(jnp.float32)
    padded_grad = extended(conv_grad, (("row", 0),), half_width).astype(jnp.float32)
    outer_masks = tap_masks(
        row_start - half_width + jnp.arange(row_count + 2 * half_width, dtype=jnp.int32)
    )
    glu_grad = jnp.zeros((row_count, chan_count), jnp.float32)
    kernel_rows = []
    for tap_index in range(K):
        begin = 2 * half_width - tap_index
        glu_grad = (
            glu_grad
            + kernel[tap_index][None, :]
            * outer_masks[tap_index, begin : begin + row_count][:, None]
            * padded_grad[begin : begin + row_count]
        )
        kernel_rows.append(
            jnp.sum(
                local_masks[tap_index][:, None]
                * conv_wide
                * padded_glu[tap_index : tap_index + row_count],
                axis=0,
            )
        )
    kernel_term = jnp.stack(kernel_rows)
    bias_term = jnp.sum(conv_wide, axis=0)
    grad_kernel, grad_bias = lax.psum((kernel_term, bias_term), "row")
    value_grad = (glu_grad * gate_sig).astype(jnp.bfloat16)
    gate_grad = (glu_grad * value_pre * gate_sig * (1.0 - gate_sig)).astype(jnp.bfloat16)
    both_grads = jnp.concatenate([value_grad, gate_grad], axis=1)
    in_weight = lax.psum_scatter(
        contract_rows(normed, both_grads).astype(jnp.bfloat16),
        "row",
        scatter_dimension=0,
        tiled=True,
    ).astype(jnp.float32)
    grad_value = in_weight[:, :chan_count]
    grad_gate = in_weight[:, chan_count:]
    norm_terms = contract_cols(value_grad, value_full) + contract_cols(gate_grad, gate_full)
    normed_grad = lax.psum_scatter(
        norm_terms.astype(jnp.bfloat16), "col", scatter_dimension=1, tiled=True
    ).astype(jnp.float32)
    hat_grad = normed_grad * local_gain[None, :]
    first_sum, second_sum = lax.psum(
        (jnp.sum(hat_grad, axis=1), jnp.sum(hat_grad * centred, axis=1)), "col"
    )
    input_grad = (
        grad_out.astype(jnp.float32)
        + inv_std[:, None]
        * (hat_grad - first_sum[:, None] / width - centred * (second_sum / width)[:, None])
    ).astype(jnp.bfloat16)
    gain_term = jnp.sum(normed_grad * centred, axis=0)
    grad_gain = lax.psum(gain_term, "row")
    return (
        encoded,
        input_grad,
        grad_value,
        grad_gate,
        grad_kernel,
        grad_bias,
        grad_out_weight,
        grad_gain,
    )


def choose(frames, gain, w_value, *others):
    fits = w_value.shape[1] % (128 * lax.axis_size("row")) == 0 and lax.axis_size("col") % lax.axis_size("row") == 0
    return (shards if fits else narrow_shards)(frames, gain, w_value, *others)


def solution(mesh):
    tile = P("row", "col")
    return jax.shard_map(
        choose,
        mesh=mesh,
        in_specs=(tile, P(), tile, tile, P(None, "col"), P("col"), tile, tile),
        out_specs=(tile, tile, tile, tile, P(None, "col"), P("col"), tile, P("col")),
        check_vma=False,
    )
```
